256 devices in a mesh: dp: 8 (over z_lo, x), dap: 32 (over y, z_hi, core).
Axes of the slice: x: 4, y: 4, z: 8 (z_hi: 4, z_lo: 2; z = z_hi * 2 + z_lo), core: 2. Of those that a mesh axis runs over, the one named last changes fastest.
Arguments:
- pair: float32 [8, 192, 192, 128], P('dp', 'dap'), may hold values from -6 to 6
- upstream: float32 [8, 192, 192, 128], P('dp', 'dap'), may hold values from -6 to 6
- residue_mask: int32 [8, 192], P('dp'), may hold values 0 or 1
- w_in: float32 [128, 512], replicated, may hold values from -0.5 to 0.5
- w_gate: float32 [128, 128], replicated, may hold values from -0.5 to 0.5
- w_out: float32 [128, 128], replicated, may hold values from -0.5 to 0.5
- gains: float32 [2, 128], replicated, may hold values from 0.5 to 1.5
Outputs:
- d_pair: float32 [8, 192, 192, 128], P('dp', 'dap')
- d_w_in: float32 [128, 512], replicated
- d_w_gate: float32 [128, 128], replicated
- d_w_out: float32 [128, 128], replicated
- d_gains: float32 [2, 128], replicated
The draws below stay inside these ranges and needn't reach their ends.
All inputs are finite; a program needn't handle non-finite values. No bound on the sum of `residue_mask` on one device may be relied on, other than what follows from the above.
Results may differ from the reference program's by a relative error of at most 0.000082.
Values sent between devices are 32-bit elements; how exact they have to be, the bound alone decides.
No kernel may reach another device: no remote copies, remote signals or barrier semaphores. Data moves between devices by JAX's collectives and lax.ppermute only.
A program may use at most 192 MiB of HBM per device.

```python
import jax
import jax.numpy as jnp
from jax import lax

C = 128
H = 128
RES = 192
SAMPLES = 8


def place_ends(entries, rng, low, high):
    longest = entries.shape.index(max(entries.shape))
    spots = []
    for shift in (0, 1):
        where = [jax.random.randint(jax.random.fold_in(rng, axis), (), 0, length) for axis, length in enumerate(entries.shape)]
        where[longest] = (where[longest] + shift) % entries.shape[longest]
        spots.append(tuple(where))
    return entries.at[spots[0]].set(low).at[spots[1]].set(high)


def shard_levels(stream_key, shape, pieces, low, largest):
    factor_of, own = 1.0, jax.random.fold_in(stream_key, 6)
    for dim, blocks in pieces:
        steps = jnp.exp(jax.random.uniform(jax.random.fold_in(own, dim), (blocks,), jnp.float32, low / len(pieces), largest / len(pieces)))
        factor_of = factor_of * jnp.repeat(steps, shape[dim] // blocks).reshape([-1 if axis == dim else 1 for axis in range(len(shape))])
    return factor_of


def centred(own_key, shape, deviation, most, cuts=(), held_as=jnp.bfloat16):
    drawn = jax.random.normal(own_key, shape, jnp.float32) * deviation
    if len(cuts) > 0:
        drawn = shard_levels(own_key, shape, cuts, -0.22, 0.18) * drawn
    return jnp.clip(drawn, min=-most, max=most).astype(held_as)


def setup_inputs(seed: int = 0) -> dict:
    arg_keys = jax.random.split(jax.random.key(seed), 8)
    pair = centred(arg_keys[0], (SAMPLES, RES, RES, C), 1.0, 6.0, ((0, 8), (1, 32)), jnp.float32)
    upstream = centred(arg_keys[1], (SAMPLES, RES, RES, C), 1.0, 6.0, ((0, 8), (1, 32)), jnp.float32)
    residue_mask = place_ends((jax.random.randint(arg_keys[2], (SAMPLES, RES), 0, 8) < 7).astype(jnp.int32), jax.random.fold_in(arg_keys[2], 1), 0, 1)
    w_in = centred(arg_keys[3], (C, 4 * H), C ** -0.5, 0.5, (), jnp.float32)
    w_gate = centred(arg_keys[4], (C, C), C ** -0.5, 0.5, (), jnp.float32)
    w_out = centred(arg_keys[5], (H, C), H ** -0.5, 0.5, (), jnp.float32)
    gains = jnp.clip(1.0 + 0.1 * jax.random.normal(arg_keys[6], (2, C), jnp.float32), 0.5, 1.5)
    return dict(pair=pair, upstream=upstream, residue_mask=residue_mask, w_in=w_in, w_gate=w_gate, w_out=w_out, gains=gains)


HIGH = lax.Precision.HIGHEST

def normed(values, gain):
    center = values - lax.optimization_barrier(jnp.mean(values, axis=-1, keepdims=True))
    spread = lax.optimization_barrier(jnp.mean(center * center, axis=-1, keepdims=True))
    return center * lax.rsqrt(spread + 1e-05) * gain

def forward(pair, w_in, w_gate, w_out, gains, pairmask):
    width = w_out.shape[0]
    zn = normed(pair, gains[0])
    proj = jnp.einsum('sijc,cf->sijf', zn, w_in, precision=HIGH)
    a_val = pairmask * jax.nn.sigmoid(proj[..., width:2 * width]) * proj[..., :width]
    b_val = pairmask * jax.nn.sigmoid(proj[..., 3 * width:]) * proj[..., 2 * width:3 * width]
    triangle_product = jnp.einsum('sikh,sjkh->sijh', a_val, b_val, precision=HIGH)
    normed_input = normed(triangle_product, gains[1])
    proj_out = jnp.einsum('sijh,hc->sijc', normed_input, w_out, precision=HIGH)
    gate = jax.nn.sigmoid(jnp.einsum('sijc,cd->sijd', zn, w_gate, precision=HIGH))
    return gate * proj_out

def reference(pair, upstream, residue_mask, w_in, w_gate, w_out, gains):
    maskf = residue_mask.astype(jnp.float32)
    pairmask = (maskf[:, :, None] * maskf[:, None, :])[..., None]

    def apply(p, wi, wg, wo, gn):
        return forward(p, wi, wg, wo, gn, pairmask)
    result, pullback = jax.vjp(apply, pair, w_in, w_gate, w_out, gains)
    d_pair, d_w_in, d_w_gate, d_w_out, d_gains = pullback(upstream)
    return (d_pair, d_w_in, d_w_gate, d_w_out, d_gains)
```

```python
import functools

import jax
import jax.numpy as jnp
from jax import lax
from jax.experimental import pallas as pl
from jax.experimental.pallas import tpu as pltpu
from jax.sharding import PartitionSpec as P

F32 = jnp.float32
BF16 = jnp.bfloat16
LANES = 384
EPS = 1e-05


def parts(x):
    hi = x.astype(BF16)
    return hi, (x - hi.astype(F32)).astype(BF16)


def dot3(left, right, dims=((1,), (0,))):
    (ah, al), (bh, bl) = left, right

    def one(a, b):
        return lax.dot_general(a, b, (dims, ((), ())), preferred_element_type=F32)

    return one(ah, bh) + (one(ah, bl) + one(al, bh))


NT = ((1,), (1,))
TN = ((0,), (0,))


def column(row):
    n = row.shape[1]
    return jnp.broadcast_to(row, (n, n)).T[:, :1]


def hat(x):
    center = x - jnp.mean(x, axis=0, keepdims=True)
    inverse = lax.rsqrt(jnp.mean(center * center, axis=0, keepdims=True) + EPS)
    return center * inverse, inverse


def hat_back(g, xhat, inverse):
    first = jnp.mean(g, axis=0, keepdims=True)
    second = jnp.mean(g * xhat, axis=0, keepdims=True)
    return inverse * (g - first - xhat * second)


def call(body, outs, scratch=(), flops=0, moved=0):
    return pl.pallas_call(
        body,
        out_shape=[jax.ShapeDtypeStruct(s, d) for s, d in outs],
        scratch_shapes=list(scratch),
        compiler_params=pltpu.CompilerParams(vmem_limit_bytes=40 * 2**20),
        cost_estimate=pl.CostEstimate(flops=flops, bytes_accessed=moved, transcendentals=0),
    )


def cell_slices(c, res):
    base = pl.multiple_of(c * 2 * res, 2 * res)
    return (
        pl.ds(base, 128),
        pl.ds(base + 128, res - 128),
        pl.ds(base + res + 128, res - 128),
        pl.ds(base + res, 128),
    )


def load_cells(ref, c, res):
    return jnp.concatenate([ref[at, :] for at in cell_slices(c, res)], axis=0).T


def store_cells(ref, c, res, value):
    value = value.T
    start = 0
    for at in cell_slices(c, res):
        ref[at, :] = value[start : start + at.size, :]
        start += at.size


def tile_rows(n, kinds, tile, kind):
    return pl.ds(tile * kinds + kind, n, stride=9 * kinds)


def to_rows(tiles):
    return (tiles[0], tiles[1]), (tiles[2], pltpu.roll(tiles[1], 64, 1))


def to_tiles(even, odd):
    low = lax.broadcasted_iota(jnp.int32, even[1].shape, 1) < 64
    return even[0], jnp.where(low, even[1], pltpu.roll(odd[1], 64, 1)), odd[0]


def project_kernel(n, res, pair, w_in, gains, send, zhat, zinv, val, sig, wt_hi, wt_lo):
    hidden = w_in.shape[1] // 4
    per = hidden // n
    wh, wl = parts(w_in[...].T)
    wt_hi[...], wt_lo[...] = wh, wl
    gain = column(gains[0:1, :])

    def step(c, _):
        at = pl.ds(pl.multiple_of(c * LANES, LANES), LANES)
        z, inverse = hat(load_cells(pair, c, res))
        zhat[:, at] = z
        zinv[:, at] = inverse
        zn = parts(z * gain)
        for which in range(2):
            rows = pl.ds(2 * which * hidden, hidden)
            gate_rows = pl.ds((2 * which + 1) * hidden, hidden)
            value = dot3((wt_hi[rows, :], wt_lo[rows, :]), zn)
            gate = jax.nn.sigmoid(dot3((wt_hi[gate_rows, :], wt_lo[gate_rows, :]), zn))
            val[pl.ds(which * hidden, hidden), at] = value
            sig[pl.ds(which * hidden, hidden), at] = gate
            both = value * gate
            for q in range(per):
                for t in range(3):
                    send[tile_rows(n, 2 * per, 3 * c + t, which * per + q), :] = both[
                        q * n : (q + 1) * n, t * 128 : (t + 1) * 128
                    ]
        return 0

    lax.fori_loop(0, pair.shape[0] // LANES, step, 0)


def make_masks(mask, line, swap, rows):
    res = mask.shape[1]
    line[...] = jnp.zeros_like(line)
    line[0:1, pl.ds(0, res)] = mask[...].astype(F32)
    across = jnp.broadcast_to(line[0:1, :], (256, 256))
    both = across * across.T
    swap[0:256, :] = both[:, :128]
    swap[256:512, :] = both[:, 128:]
    n = res // rows
    return [[swap[pl.ds(256 * half + il, n, stride=rows), :] for half in range(2)] for il in range(rows)]


MASK_SCRATCH = [pltpu.VMEM((8, 256), F32), pltpu.VMEM((512, 128), F32)]


def triangle_kernel(n, got, mask, send, a_out, b_out, line, swap):
    per = got.shape[0] // (2 * 9 * n)
    res = mask.shape[1]
    rows = res // n
    pm = make_masks(mask, line, swap, rows)
    for q in range(per):
        base = 512 * q
        for half in range(2):
            b_out[pl.ds(base + 256 * half + res, 256 - res), :] = jnp.zeros((256 - res, 128), F32)
        for p in range(rows // 2):
            two_a = to_rows([got[tile_rows(n, 2 * per, 3 * p + t, q), :] for t in range(3)])
            two_b = to_rows([got[tile_rows(n, 2 * per, 3 * p + t, per + q), :] for t in range(3)])
            for side in range(2):
                il = 2 * p + side
                for half in range(2):
                    a_out[q, pl.ds(il * n, n), pl.ds(128 * half, 128)] = two_a[side][half] * pm[il][half]
                    b_out[pl.ds(base + 256 * half + il, n, stride=rows), :] = two_b[side][half] * pm[il][half]
        b_whole = jnp.concatenate([b_out[pl.ds(base, 256), :], b_out[pl.ds(base + 256, 256), :]], axis=1)
        x = dot3(parts(a_out[q]), parts(b_whole), NT)
        for p in range(rows // 2):
            even, odd = [
                [x[(2 * p + side) * n : (2 * p + side + 1) * n, 128 * half : 128 * half + 128] for half in range(2)]
                for side in range(2)
            ]
            for t, tile in enumerate(to_tiles(even, odd)):
                send[tile_rows(n, per, 3 * p + t, q), :] = tile


def output_kernel(n, res, got, up, zhat, w_gate, w_out, gains, send, dzn, mg, mo, wgt, wot):
    hidden = w_out.shape[0]
    per = hidden // n
    gain0, gain1 = column(gains[0:1, :]), column(gains[1:2, :])
    wgt[...] = w_gate[...].T
    wot[...] = w_out[...].T
    mg[...] = jnp.zeros_like(mg)
    mo[...] = jnp.zeros_like(mo)

    def step(c, _):
        at = pl.ds(pl.multiple_of(c * LANES, LANES), LANES)
        x = jnp.concatenate(
            [
                jnp.concatenate([got[tile_rows(n, per, 3 * c + t, q), :] for q in range(per)], axis=0)
                for t in range(3)
            ],
            axis=1,
        )
        xhat, inverse = hat(x)
        z = zhat[:, at]
        z_parts = parts(z)
        upstream = load_cells(up, c, res)
        gate = jax.nn.sigmoid(dot3(parts(wgt[...]), parts(z * gain0)))
        out = dot3(parts(wot[...]), parts(xhat * gain1))
        d_out = parts(upstream * gate)
        d_logit = parts(upstream * out * gate * (1.0 - gate))
        mo[...] += dot3(d_out, parts(xhat), NT)
        mg[...] += dot3(d_logit, z_parts, NT)
        dzn[:, at] = dot3(parts(w_gate[...]), d_logit)
        g = dot3(parts(w_out[...]), d_out) * gain1
        dx = hat_back(g, xhat, inverse)
        for q in range(per):
            for t in range(3):
                send[tile_rows(n, per, 3 * c + t, q), :] = dx[q * n : (q + 1) * n, t * 128 : (t + 1) * 128]
        return 0

    lax.fori_loop(0, up.shape[0] // LANES, step, 0)


def triangle_back_kernel(n, got, mask, a_in, b_in, send, line, swap, dx_all, db_all):
    per = got.shape[0] // (9 * n)
    res = mask.shape[1]
    rows = res // n
    pm = make_masks(mask, line, swap, rows)
    for q in range(per):
        base = 512 * q
        for p in range(rows // 2):
            two = to_rows([got[tile_rows(n, per, 3 * p + t, q), :] for t in range(3)])
            for side in range(2):
                for half in range(2):
                    dx_all[pl.ds((2 * p + side) * n, n), pl.ds(128 * half, 128)] = two[side][half]
        dx = parts(dx_all[...])
        b_whole = jnp.concatenate([b_in[pl.ds(base, 256), :], b_in[pl.ds(base + 256, 256), :]], axis=1)
        da = dot3(dx, parts(b_whole))
        db = dot3(dx, parts(a_in[q]), TN)
        db_all[0:256, :] = db[:, :128]
        db_all[256:512, :] = db[:, 128:]
        for p in range(rows // 2):
            two_a, two_b = [], []
            for il in (2 * p, 2 * p + 1):
                two_a.append([da[il * n : (il + 1) * n, 128 * half : 128 * half + 128] * pm[il][half] for half in range(2)])
                two_b.append([db_all[pl.ds(256 * half + il, n, stride=rows), :] * pm[il][half] for half in range(2)])
            for t, tile in enumerate(to_tiles(*two_a)):
                send[tile_rows(n, 2 * per, 3 * p + t, q), :] = tile
            for t, tile in enumerate(to_tiles(*two_b)):
                send[tile_rows(n, 2 * per, 3 * p + t, per + q), :] = tile


def input_kernel(n, res, got, zhat, zinv, val, sig, dzn, w_in, gains, d_pair, mi, w_hi, w_lo):
    hidden = w_in.shape[1] // 4
    per = hidden // n
    wh, wl = parts(w_in[...])
    w_hi[...], w_lo[...] = wh, wl
    gain0 = column(gains[0:1, :])
    mi[...] = jnp.zeros_like(mi)

    def step(c, _):
        at = pl.ds(pl.multiple_of(c * LANES, LANES), LANES)
        z = zhat[:, at]
        z_parts = parts(z)
        total = dzn[:, at]
        for which in range(2):
            d = jnp.concatenate(
                [
                    jnp.concatenate(
                        [got[tile_rows(n, 2 * per, 3 * c + t, which * per + q), :] for q in range(per)], axis=0
                    )
                    for t in range(3)
                ],
                axis=1,
            )
            rows = pl.ds(which * hidden, hidden)
            gate = sig[rows, at]
            d_val = d * gate
            d_gate = d_val * val[rows, at] * (1.0 - gate)
            for k, grad in ((2 * which, d_val), (2 * which + 1, d_gate)):
                cols = pl.ds(k * hidden, hidden)
                grad = parts(grad)
                total += dot3((w_hi[:, cols], w_lo[:, cols]), grad)
                mi[cols, :] += dot3(grad, z_parts, NT)
        store_cells(d_pair, c, res, hat_back(total * gain0, z, zinv[:, at]))
        return 0

    lax.fori_loop(0, d_pair.shape[0] // LANES, step, 0)


def finish_kernel(m, w_in, w_gate, w_out, gains, d_w_in, d_w_gate, d_w_out, d_gains):
    width = w_out.shape[0]
    gain0, gain1 = column(gains[0:1, :]), column(gains[1:2, :])
    fold = jnp.zeros((width, width), F32)
    for k in range(w_in.shape[1] // width):
        cols = pl.ds(k * width, width)
        part = m[cols, :].T
        d_w_in[:, cols] = part * gain0
        fold += part * w_in[:, cols]
    base = w_in.shape[1]
    part = m[pl.ds(base, width), :].T
    d_w_gate[...] = part * gain0
    fold += part * w_gate[...]
    d_gains[0:1, :] = jnp.sum(fold.T, axis=0, keepdims=True)
    part = m[pl.ds(base + width, width), :].T
    d_w_out[...] = part * gain1
    d_gains[1:2, :] = jnp.sum((part * w_out[...]).T, axis=0, keepdims=True)


def exchange(x, axis):
    return lax.all_to_all(x, axis, 0, 0, tiled=True)


def shards(n, n_dp, pair, upstream, residue_mask, w_in, w_gate, w_out, gains):
    _, rows, res, width = pair.shape
    hidden = w_out.shape[0]
    cells = rows * res
    per = hidden // n
    pair2 = pair.reshape(cells, width)
    up2 = upstream.reshape(cells, width)
    tiles = n * 9 * per

    def wide(x):
        return exchange(x.reshape(n, 18 * per, 128), "dap").reshape(2 * tiles, 128)

    def narrow(x):
        return exchange(x.reshape(n * 9, per, 128), "dap").reshape(tiles, 128)

    send, zhat, zinv, val, sig = call(
        functools.partial(project_kernel, n, res),
        [
            ((2 * tiles, 128), F32),
            ((width, cells), F32),
            ((1, cells), F32),
            ((2 * hidden, cells), F32),
            ((2 * hidden, cells), F32),
        ],
        [pltpu.VMEM((4 * hidden, width), BF16)] * 2,
    )(pair2, w_in, gains)
    got = wide(send)

    send, a_all, b_all = call(
        functools.partial(triangle_kernel, n),
        [((tiles, 128), F32), ((per, res, 256), F32), ((per * 512, 128), F32)],
        MASK_SCRATCH,
    )(got, residue_mask)
    got = narrow(send)

    send, dzn, mg, mo = call(
        functools.partial(output_kernel, n, res),
        [
            ((tiles, 128), F32),
            ((width, cells), F32),
            ((width, width), F32),
            ((width, hidden), F32),
        ],
        [pltpu.VMEM((width, width), F32), pltpu.VMEM((width, hidden), F32)],
    )(got, up2, zhat, w_gate, w_out, gains)
    got = narrow(send)

    (send,) = call(
        functools.partial(triangle_back_kernel, n),
        [((2 * tiles, 128), F32)],
        MASK_SCRATCH + [pltpu.VMEM((res, 256), F32), pltpu.VMEM((512, 128), F32)],
    )(got, residue_mask, a_all, b_all)
    got = wide(send)

    d_pair, mi = call(
        functools.partial(input_kernel, n, res),
        [((cells, width), F32), ((4 * hidden, width), F32)],
        [pltpu.VMEM((width, 4 * hidden), BF16)] * 2,
    )(got, zhat, zinv, val, sig, dzn, w_in, gains)

    m = jnp.concatenate([mi, mg, mo], axis=0)
    count = m.shape[0]
    mine = jnp.sum(exchange(m.reshape(n, count // n, width), "dap"), axis=0)
    mine = jnp.broadcast_to(mine[None], (n_dp,) + mine.shape)
    mine = jnp.sum(exchange(mine, "dp"), axis=0)
    m = exchange(jnp.broadcast_to(mine[None], (n,) + mine.shape), "dap").reshape(count, width)

    d_w_in, d_w_gate, d_w_out, d_gains = call(
        finish_kernel,
        [(w_in.shape, F32), (w_gate.shape, F32), (w_out.shape, F32), (gains.shape, F32)],
    )(m, w_in, w_gate, w_out, gains)
    return (d_pair.reshape(pair.shape), d_w_in, d_w_gate, d_w_out, d_gains)


def solution(mesh):
    cells = P("dp", "dap", None, None)
    in_specs = (cells, cells, P("dp", None), P(), P(), P(), P())
    out_specs = (cells, P(), P(), P(), P())
    body = functools.partial(shards, mesh.shape["dap"], mesh.shape["dp"])
    return jax.shard_map(body, mesh=mesh, in_specs=in_specs, out_specs=out_specs, check_vma=False)
```

```python
import functools

import jax
import jax.numpy as jnp
from jax import lax
from jax.experimental import pallas as pl
from jax.experimental.pallas import tpu as pltpu
from jax.sharding import PartitionSpec as P

F32 = jnp.float32
BF16 = jnp.bfloat16
LANES = 384
EPS = 1e-05


def parts(x):
    hi = x.astype(BF16)
    return hi, (x - hi.astype(F32)).astype(BF16)


def dot3(left, right, dims=((1,), (0,))):
    (ah, al), (bh, bl) = left, right

    def one(a, b):
        return lax.dot_general(a, b, (dims, ((), ())), preferred_element_type=F32)

    return one(ah, bh) + (one(ah, bl) + one(al, bh))


NT = ((1,), (1,))
TN = ((0,), (0,))


def column(row):
    n = row.shape[1]
    return jnp.broadcast_to(row, (n, n)).T[:, :1]


def hat(x):
    center = x - jnp.mean(x, axis=0, keepdims=True)
    inverse = lax.rsqrt(jnp.mean(center * center, axis=0, keepdims=True) + EPS)
    return center * inverse, inverse


def hat_back(g, xhat, inverse):
    first = jnp.mean(g, axis=0, keepdims=True)
    second = jnp.mean(g * xhat, axis=0, keepdims=True)
    return inverse * (g - first - xhat * second)


def call(body, outs, scratch=(), flops=0, moved=0):
    return pl.pallas_call(
        body,
        out_shape=[jax.ShapeDtypeStruct(s, d) for s, d in outs],
        scratch_shapes=list(scratch),
        compiler_params=pltpu.CompilerParams(vmem_limit_bytes=40 * 2**20),
        cost_estimate=pl.CostEstimate(flops=flops, bytes_accessed=moved, transcendentals=0),
    )


def cell_slices(c, res):
    base = pl.multiple_of(c * 2 * res, 2 * res)
    return (
        pl.ds(base, 128),
        pl.ds(base + 128, res - 128),
        pl.ds(base + res + 128, res - 128),
        pl.ds(base + res, 128),
    )


def load_cells(ref, c, res):
    return jnp.concatenate([ref[at, :] for at in cell_slices(c, res)], axis=0).T


def store_cells(ref, c, res, value):
    value = value.T
    start = 0
    for at in cell_slices(c, res):
        ref[at, :] = value[start : start + at.size, :]
        start += at.size


def tile_rows(n, kinds, tile, kind):
    return pl.ds(tile * kinds + kind, n, stride=9 * kinds)


def to_rows(tiles):
    return (tiles[0], tiles[1]), (tiles[2], pltpu.roll(tiles[1], 64, 1))


def to_tiles(even, odd):
    low = lax.broadcasted_iota(jnp.int32, even[1].shape, 1) < 64
    return even[0], jnp.where(low, even[1], pltpu.roll(odd[1], 64, 1)), odd[0]


def project_kernel(n, res, pair, w_in, gains, send, zhat, zinv, val, sig, wt_hi, wt_lo):
    hidden = w_in.shape[1] // 4
    per = hidden // n
    wh, wl = parts(w_in[...].T)
    wt_hi[...], wt_lo[...] = wh, wl
    gain = column(gains[0:1, :])

    def step(c, _):
        at = pl.ds(pl.multiple_of(c * LANES, LANES), LANES)
        z, inverse = hat(load_cells(pair, c, res))
        zhat[:, at] = z
        zinv[:, at] = inverse
        zn = parts(z * gain)
        for which in range(2):
            rows = pl.ds(2 * which * hidden, hidden)
            gate_rows = pl.ds((2 * which + 1) * hidden, hidden)
            value = dot3((wt_hi[rows, :], wt_lo[rows, :]), zn)
            gate = jax.nn.sigmoid(dot3((wt_hi[gate_rows, :], wt_lo[gate_rows, :]), zn))
            val[pl.ds(which * hidden, hidden), at] = value
            sig[pl.ds(which * hidden, hidden), at] = gate
            both = value * gate
            for q in range(per):
                for t in range(3):
                    send[tile_rows(n, 2 * per, 3 * c + t, which * per + q), :] = both[
                        q * n : (q + 1) * n, t * 128 : (t + 1) * 128
                    ]
        return 0

    lax.fori_loop(0, pair.shape[0] // LANES, step, 0)


def make_masks(mask, line, swap, n):
    res = mask.shape[1]
    line[...] = jnp.zeros_like(line)
    line[0:1, pl.ds(0, res)] = mask[...].astype(F32)
    across = jnp.broadcast_to(line[0:1, :], (256, 256))
    both = across * across.T
    swap[0:256, :] = both[:, :128]
    swap[256:512, :] = both[:, 128:]
    rows = res // n
    return [[swap[pl.ds(256 * half + il, n, stride=rows), :] for half in range(2)] for il in range(rows)]


MASK_SCRATCH = [pltpu.VMEM((8, 256), F32), pltpu.VMEM((512, 128), F32)]


def core_of():
    return lax.rem(lax.axis_index("dap"), 2)


def by_core(mine, other):
    first = core_of() == 0
    return jnp.where(first, mine, other), jnp.where(first, other, mine)


def triangle_kernel(n, got, other, mask, send, a_out, b_out, line, swap):
    per = got.shape[0] // (2 * 9 * n)
    res = mask.shape[1]
    rows = res // (2 * n)
    pm = make_masks(mask, line, swap, n)
    for q in range(per):
        base = 512 * q
        for half in range(2):
            b_out[pl.ds(base + 256 * half + res, 256 - res), :] = jnp.zeros((256 - res, 128), F32)
        for p in range(rows // 2):
            two_a = to_rows([got[tile_rows(n, 2 * per, 3 * p + t, q), :] for t in range(3)])
            mine = [got[tile_rows(n, 2 * per, 3 * p + t, per + q), :] for t in range(3)]
            theirs = [other[tile_rows(n, per, 3 * p + t, q), :] for t in range(3)]
            tiles = [by_core(m, o) for m, o in zip(mine, theirs)]
            two_b = [to_rows([tile[core] for tile in tiles]) for core in range(2)]
            for side in range(2):
                il = 2 * p + side
                for half in range(2):
                    own = by_core(*[pm[core * rows + il][half] for core in range(2)])[0]
                    a_out[q, pl.ds(il * n, n), pl.ds(128 * half, 128)] = two_a[side][half] * own
                    for core in range(2):
                        row = core * rows + il
                        b_out[pl.ds(base + 256 * half + row, n, stride=2 * rows), :] = (
                            two_b[core][side][half] * pm[row][half]
                        )
        b_whole = jnp.concatenate([b_out[pl.ds(base, 256), :], b_out[pl.ds(base + 256, 256), :]], axis=1)
        x = dot3(parts(a_out[q]), parts(b_whole), NT)
        for p in range(rows // 2):
            even, odd = [
                [x[(2 * p + side) * n : (2 * p + side + 1) * n, 128 * half : 128 * half + 128] for half in range(2)]
                for side in range(2)
            ]
            for t, tile in enumerate(to_tiles(even, odd)):
                send[tile_rows(n, per, 3 * p + t, q), :] = tile


def output_kernel(n, res, got, up, zhat, w_gate, w_out, gains, send, dzn, mg, mo, wgt, wot):
    hidden = w_out.shape[0]
    per = hidden // n
    gain0, gain1 = column(gains[0:1, :]), column(gains[1:2, :])
    wgt[...] = w_gate[...].T
    wot[...] = w_out[...].T
    mg[...] = jnp.zeros_like(mg)
    mo[...] = jnp.zeros_like(mo)

    def step(c, _):
        at = pl.ds(pl.multiple_of(c * LANES, LANES), LANES)
        x = jnp.concatenate(
            [
                jnp.concatenate([got[tile_rows(n, per, 3 * c + t, q), :] for q in range(per)], axis=0)
                for t in range(3)
            ],
            axis=1,
        )
        xhat, inverse = hat(x)
        z = zhat[:, at]
        z_parts = parts(z)
        upstream = load_cells(up, c, res)
        gate = jax.nn.sigmoid(dot3(parts(wgt[...]), parts(z * gain0)))
        out = dot3(parts(wot[...]), parts(xhat * gain1))
        d_out = parts(upstream * gate)
        d_logit = parts(upstream * out * gate * (1.0 - gate))
        mo[...] += dot3(d_out, parts(xhat), NT)
        mg[...] += dot3(d_logit, z_parts, NT)
        dzn[:, at] = dot3(parts(w_gate[...]), d_logit)
        g = dot3(parts(w_out[...]), d_out) * gain1
        dx = hat_back(g, xhat, inverse)
        for q in range(per):
            for t in range(3):
                send[tile_rows(n, per, 3 * c + t, q), :] = dx[q * n : (q + 1) * n, t * 128 : (t + 1) * 128]
        return 0

    lax.fori_loop(0, up.shape[0] // LANES, step, 0)


def gather_dx(n, got, q, dx_all):
    per = got.shape[0] // (9 * n)
    for p in range(3):
        two = to_rows([got[tile_rows(n, per, 3 * p + t, q), :] for t in range(3)])
        for side in range(2):
            for half in range(2):
                dx_all[pl.ds((2 * p + side) * n, n), pl.ds(128 * half, 128)] = two[side][half]
    return parts(dx_all[...])


def b_back_kernel(n, got, mask, a_in, keep, give, line, swap, dx_all, db_all):
    per = got.shape[0] // (9 * n)
    res = mask.shape[1]
    rows = res // (2 * n)
    pm = make_masks(mask, line, swap, n)
    for q in range(per):
        db = dot3(gather_dx(n, got, q, dx_all), parts(a_in[q]), TN)
        db_all[0:256, :] = db[:, :128]
        db_all[256:512, :] = db[:, 128:]
        for p in range(rows // 2):
            tiles = []
            for core in range(2):
                two = []
                for row in (core * rows + 2 * p, core * rows + 2 * p + 1):
                    two.append(
                        [db_all[pl.ds(256 * half + row, n, stride=2 * rows), :] * pm[row][half] for half in range(2)]
                    )
                tiles.append(to_tiles(*two))
            for t in range(3):
                at = tile_rows(n, per, 3 * p + t, q)
                keep[at, :], give[at, :] = by_core(tiles[0][t], tiles[1][t])


def a_back_kernel(n, got, mask, b_in, keep, taken, send, line, swap, dx_all):
    per = got.shape[0] // (9 * n)
    res = mask.shape[1]
    rows = res // (2 * n)
    pm = make_masks(mask, line, swap, n)
    for q in range(per):
        base = 512 * q
        b_whole = jnp.concatenate([b_in[pl.ds(base, 256), :], b_in[pl.ds(base + 256, 256), :]], axis=1)
        da = dot3(gather_dx(n, got, q, dx_all), parts(b_whole))
        for p in range(rows // 2):
            two = []
            for il in (2 * p, 2 * p + 1):
                own = [by_core(pm[il][half], pm[rows + il][half])[0] for half in range(2)]
                two.append([da[il * n : (il + 1) * n, 128 * half : 128 * half + 128] * own[half] for half in range(2)])
            for t, tile in enumerate(to_tiles(*two)):
                at = tile_rows(n, per, 3 * p + t, q)
                send[tile_rows(n, 2 * per, 3 * p + t, q), :] = tile
                send[tile_rows(n, 2 * per, 3 * p + t, per + q), :] = keep[at, :] + taken[at, :]


def input_kernel(n, res, got, zhat, zinv, val, sig, dzn, w_in, gains, mg, mo, d_pair, keep, give, mi, w_hi, w_lo):
    hidden = w_in.shape[1] // 4
    per = hidden // n
    wh, wl = parts(w_in[...])
    w_hi[...], w_lo[...] = wh, wl
    gain0 = column(gains[0:1, :])
    mi[...] = jnp.zeros_like(mi)

    def step(c, _):
        at = pl.ds(pl.multiple_of(c * LANES, LANES), LANES)
        z = zhat[:, at]
        z_parts = parts(z)
        total = dzn[:, at]
        for which in range(2):
            d = jnp.concatenate(
                [
                    jnp.concatenate(
                        [got[tile_rows(n, 2 * per, 3 * c + t, which * per + q), :] for q in range(per)], axis=0
                    )
                    for t in range(3)
                ],
                axis=1,
            )
            rows = pl.ds(which * hidden, hidden)
            gate = sig[rows, at]
            d_val = d * gate
            d_gate = d_val * val[rows, at] * (1.0 - gate)
            for k, grad in ((2 * which, d_val), (2 * which + 1, d_gate)):
                cols = pl.ds(k * hidden, hidden)
                grad = parts(grad)
                total += dot3((w_hi[:, cols], w_lo[:, cols]), grad)
                mi[cols, :] += dot3(grad, z_parts, NT)
        store_cells(d_pair, c, res, hat_back(total * gain0, z, zinv[:, at]))
        return 0

    lax.fori_loop(0, d_pair.shape[0] // LANES, step, 0)
    half = keep.shape[0]
    low = mi[pl.ds(0, half), :]
    high = jnp.concatenate([mi[pl.ds(half, mi.shape[0] - half), :], mg[...], mo[...]], axis=0)
    keep[...], give[...] = by_core(low, high)


def finish_kernel(mine, theirs, w_in, w_gate, w_out, gains, d_w_in, d_w_gate, d_w_out, d_gains, m):
    width = w_out.shape[0]
    half = mine.shape[0]
    m[0:half, :], m[half:, :] = by_core(mine[...], theirs[...])
    gain0, gain1 = column(gains[0:1, :]), column(gains[1:2, :])
    fold = jnp.zeros((width, width), F32)
    for k in range(w_in.shape[1] // width):
        cols = pl.ds(k * width, width)
        part = m[cols, :].T
        d_w_in[:, cols] = part * gain0
        fold += part * w_in[:, cols]
    base = w_in.shape[1]
    part = m[pl.ds(base, width), :].T
    d_w_gate[...] = part * gain0
    fold += part * w_gate[...]
    d_gains[0:1, :] = jnp.sum(fold.T, axis=0, keepdims=True)
    part = m[pl.ds(base + width, width), :].T
    d_w_out[...] = part * gain1
    d_gains[1:2, :] = jnp.sum((part * w_out[...]).T, axis=0, keepdims=True)


def exchange(x, axis, groups):
    return lax.all_to_all(x, axis, 0, 0, tiled=True, axis_index_groups=groups)


def swap_cores(x, n):
    return lax.ppermute(x, "dap", [(i, i ^ 1) for i in range(2 * n)])


BOTH = ("dp", "dap")
NY = 4


def plane_and_line(n, n_dp):
    nx = max(1, n_dp // 2)
    nlo, nhi = n_dp // nx, n // NY

    def index(x, y, hi, lo, core):
        return (lo * nx + x) * 2 * n + (y * nhi + hi) * 2 + core

    planes = [
        [index(x, y, hi, lo, core) for x in range(nx) for y in range(NY)]
        for hi in range(nhi)
        for lo in range(nlo)
        for core in range(2)
    ]
    lines = [
        [index(x, y, hi, lo, core) for hi in range(nhi) for lo in range(nlo)]
        for x in range(nx)
        for y in range(NY)
        for core in range(2)
    ]
    return planes, lines


def reduce_all(keep, give, n, n_dp):
    planes, lines = plane_and_line(n, n_dp)
    count, width = keep.shape

    def summed(x, groups, pieces):
        return jnp.sum(exchange(x.reshape(pieces, -1, width), BOTH, groups), axis=0)

    def spread(x, pieces):
        return jnp.broadcast_to(x[None], (pieces,) + x.shape)

    in_plane, in_line = len(planes[0]), len(lines[0])
    mine = summed(keep + swap_cores(give, n), planes, in_plane)
    mine = summed(spread(mine, in_line), lines, in_line)
    mine = exchange(spread(mine, in_plane), BOTH, planes).reshape(count, width)
    return mine, swap_cores(mine, n)


def shards(devices, n_dp, pair, upstream, residue_mask, w_in, w_gate, w_out, gains):
    _, rows, res, width = pair.shape
    hidden = w_out.shape[0]
    cells = rows * res
    n = devices // 2
    per = hidden // n
    same_core = [list(range(core, devices, 2)) for core in range(2)]
    pair2 = pair.reshape(cells, width)
    up2 = upstream.reshape(cells, width)
    tiles = n * 9 * per

    def wide(x):
        return exchange(x.reshape(n, 18 * per, 128), "dap", same_core).reshape(2 * tiles, 128)

    def narrow(x):
        return exchange(x.reshape(n, 9 * per, 128), "dap", same_core).reshape(tiles, 128)

    send, zhat, zinv, val, sig = call(
        functools.partial(project_kernel, n, res),
        [
            ((2 * tiles, 128), F32),
            ((width, cells), F32),
            ((1, cells), F32),
            ((2 * hidden, cells), F32),
            ((2 * hidden, cells), F32),
        ],
        [pltpu.VMEM((4 * hidden, width), BF16)] * 2,
    )(pair2, w_in, gains)
    got = wide(send)

    other = swap_cores(got.reshape(n * 9, 2, per, 128)[:, 1].reshape(tiles, 128), n)
    send, a_all, b_all = call(
        functools.partial(triangle_kernel, n),
        [((tiles, 128), F32), ((per, res // 2, 256), F32), ((per * 512, 128), F32)],
        MASK_SCRATCH,
    )(got, other, residue_mask)
    got = narrow(send)

    send, dzn, mg, mo = call(
        functools.partial(output_kernel, n, res),
        [
            ((tiles, 128), F32),
            ((width, cells), F32),
            ((width, width), F32),
            ((width, hidden), F32),
        ],
        [pltpu.VMEM((width, width), F32), pltpu.VMEM((width, hidden), F32)],
    )(got, up2, zhat, w_gate, w_out, gains)
    got = narrow(send)

    keep, give = call(
        functools.partial(b_back_kernel, n),
        [((tiles, 128), F32)] * 2,
        MASK_SCRATCH + [pltpu.VMEM((res // 2, 256), F32), pltpu.VMEM((512, 128), F32)],
    )(got, residue_mask, a_all)
    taken = swap_cores(give, n)
    (send,) = call(
        functools.partial(a_back_kernel, n),
        [((2 * tiles, 128), F32)],
        MASK_SCRATCH + [pltpu.VMEM((res // 2, 256), F32)],
    )(got, residue_mask, b_all, keep, taken)
    got = wide(send)

    half = (4 * hidden + 2 * width) // 2
    d_pair, keep, give = call(
        functools.partial(input_kernel, n, res),
        [((cells, width), F32), ((half, width), F32), ((half, width), F32)],
        [pltpu.VMEM((4 * hidden, width), F32)] + [pltpu.VMEM((width, 4 * hidden), BF16)] * 2,
    )(got, zhat, zinv, val, sig, dzn, w_in, gains, mg, mo)
    mine, theirs = reduce_all(keep, give, n, n_dp)

    d_w_in, d_w_gate, d_w_out, d_gains = call(
        finish_kernel,
        [(w_in.shape, F32), (w_gate.shape, F32), (w_out.shape, F32), (gains.shape, F32)],
        [pltpu.VMEM((2 * half, width), F32)],
    )(mine, theirs, w_in, w_gate, w_out, gains)
    return (d_pair.reshape(pair.shape), d_w_in, d_w_gate, d_w_out, d_gains)


def solution(mesh):
    cells = P("dp", "dap", None, None)
    in_specs = (cells, cells, P("dp", None), P(), P(), P(), P())
    out_specs = (cells, P(), P(), P(), P())
    body = functools.partial(shards, mesh.shape["dap"], mesh.shape["dp"])
    return jax.shard_map(body, mesh=mesh, in_specs=in_specs, out_specs=out_specs, check_vma=False)
```

```python
import functools

import jax
import jax.numpy as jnp
from jax import lax
from jax.experimental import pallas as pl
from jax.experimental.pallas import tpu as pltpu
from jax.sharding import PartitionSpec as P

F32 = jnp.float32
BF16 = jnp.bfloat16
LANES = 384
EPS = 1e-05


def parts(x):
    hi = x.astype(BF16)
    return hi, (x - hi.astype(F32)).astype(BF16)


def dot3(left, right, dims=((1,), (0,))):
    (ah, al), (bh, bl) = left, right

    def one(a, b):
        return lax.dot_general(a, b, (dims, ((), ())), preferred_element_type=F32)

    return one(ah, bh) + (one(ah, bl) + one(al, bh))


NT = ((1,), (1,))
TN = ((0,), (0,))


def column(row):
    n = row.shape[1]
    return jnp.broadcast_to(row, (n, n)).T[:, :1]


def hat(x):
    center = x - jnp.mean(x, axis=0, keepdims=True)
    inverse = lax.rsqrt(jnp.mean(center * center, axis=0, keepdims=True) + EPS)
    return center * inverse, inverse


def hat_back(g, xhat, inverse):
    first = jnp.mean(g, axis=0, keepdims=True)
    second = jnp.mean(g * xhat, axis=0, keepdims=True)
    return inverse * (g - first - xhat * second)


def call(body, outs, scratch=(), flops=0, moved=0):
    return pl.pallas_call(
        body,
        out_shape=[jax.ShapeDtypeStruct(s, d) for s, d in outs],
        scratch_shapes=list(scratch),
        compiler_params=pltpu.CompilerParams(vmem_limit_bytes=40 * 2**20),
        cost_estimate=pl.CostEstimate(flops=flops, bytes_accessed=moved, transcendentals=0),
    )


def cell_slices(c, res):
    base = pl.multiple_of(c * 2 * res, 2 * res)
    return (
        pl.ds(base, 128),
        pl.ds(base + 128, res - 128),
        pl.ds(base + res + 128, res - 128),
        pl.ds(base + res, 128),
    )


def load_cells(ref, c, res):
    return jnp.concatenate([ref[at, :] for at in cell_slices(c, res)], axis=0).T


def store_cells(ref, c, res, value):
    value = value.T
    start = 0
    for at in cell_slices(c, res):
        ref[at, :] = value[start : start + at.size, :]
        start += at.size


def tile_rows(n, kinds, tile, kind):
    return pl.ds(tile * kinds + kind, n, stride=9 * kinds)


def to_rows(tiles):
    return (tiles[0], tiles[1]), (tiles[2], pltpu.roll(tiles[1], 64, 1))


def to_tiles(even, odd):
    low = lax.broadcasted_iota(jnp.int32, even[1].shape, 1) < 64
    return even[0], jnp.where(low, even[1], pltpu.roll(odd[1], 64, 1)), odd[0]


def project_kernel(n, res, pair, w_in, gains, send, zhat, zinv, val, sig, wt_hi, wt_lo):
    hidden = w_in.shape[1] // 4
    per = hidden // n
    wh, wl = parts(w_in[...].T)
    wt_hi[...], wt_lo[...] = wh, wl
    gain = column(gains[0:1, :])

    def step(c, _):
        at = pl.ds(pl.multiple_of(c * LANES, LANES), LANES)
        z, inverse = hat(load_cells(pair, c, res))
        zhat[:, at] = z
        zinv[:, at] = inverse
        zn = parts(z * gain)
        for which in range(2):
            rows = pl.ds(2 * which * hidden, hidden)
            gate_rows = pl.ds((2 * which + 1) * hidden, hidden)
            value = dot3((wt_hi[rows, :], wt_lo[rows, :]), zn)
            gate = jax.nn.sigmoid(dot3((wt_hi[gate_rows, :], wt_lo[gate_rows, :]), zn))
            val[pl.ds(which * hidden, hidden), at] = value
            sig[pl.ds(which * hidden, hidden), at] = gate
            both = value * gate
            for q in range(per):
                for t in range(3):
                    send[tile_rows(n, 2 * per, 3 * c + t, which * per + q), :] = both[
                        q * n : (q + 1) * n, t * 128 : (t + 1) * 128
                    ]
        return 0

    lax.fori_loop(0, pair.shape[0] // LANES, step, 0)


def make_masks(mask, line, swap):
    res = mask.shape[1]
    line[...] = jnp.zeros_like(line)
    line[0:1, pl.ds(0, res)] = mask[...].astype(F32)
    across = jnp.broadcast_to(line[0:1, :], (256, 256))
    both = across * across.T
    swap[0:256, :] = both[:, :128]
    swap[256:512, :] = both[:, 128:]


def read_masks(swap, n, res):
    rows = res // n
    return [[swap[pl.ds(256 * half + il, n, stride=rows), :] for half in range(2)] for il in range(rows)]


def core_of():
    return lax.rem(lax.axis_index("dap"), 2)


def by_core(mine, other):
    first = core_of() == 0
    return jnp.where(first, mine, other), jnp.where(first, other, mine)


def triangle_kernel(n, got, other, mask, send, a_out, b_out, swap, line):
    per = got.shape[0] // (2 * 9 * n)
    res = mask.shape[1]
    rows = res // (2 * n)
    make_masks(mask, line, swap)
    pm = read_masks(swap, n, res)
    for q in range(per):
        base = 512 * q
        for half in range(2):
            b_out[pl.ds(base + 256 * half + res, 256 - res), :] = jnp.zeros((256 - res, 128), F32)
        for p in range(rows // 2):
            two_a = to_rows([got[tile_rows(n, 2 * per, 3 * p + t, q), :] for t in range(3)])
            mine = [got[tile_rows(n, 2 * per, 3 * p + t, per + q), :] for t in range(3)]
            theirs = [other[tile_rows(n, per, 3 * p + t, q), :] for t in range(3)]
            tiles = [by_core(m, o) for m, o in zip(mine, theirs)]
            two_b = [to_rows([tile[core] for tile in tiles]) for core in range(2)]
            for side in range(2):
                il = 2 * p + side
                for half in range(2):
                    own = by_core(*[pm[core * rows + il][half] for core in range(2)])[0]
                    a_out[q, pl.ds(il * n, n), pl.ds(128 * half, 128)] = two_a[side][half] * own
                    for core in range(2):
                        row = core * rows + il
                        b_out[pl.ds(base + 256 * half + row, n, stride=2 * rows), :] = (
                            two_b[core][side][half] * pm[row][half]
                        )
        b_whole = jnp.concatenate([b_out[pl.ds(base, 256), :], b_out[pl.ds(base + 256, 256), :]], axis=1)
        x = dot3(parts(a_out[q]), parts(b_whole), NT)
        for p in range(rows // 2):
            even, odd = [
                [x[(2 * p + side) * n : (2 * p + side + 1) * n, 128 * half : 128 * half + 128] for half in range(2)]
                for side in range(2)
            ]
            for t, tile in enumerate(to_tiles(even, odd)):
                send[tile_rows(n, per, 3 * p + t, q), :] = tile


def gate_kernel(res, up, zhat, w_gate, w_out, gains, d_out, slope, grad, wgt):
    gain0, gain1 = column(gains[0:1, :]), column(gains[1:2, :])
    wgt[...] = w_gate[...].T

    def step(c, _):
        at = pl.ds(pl.multiple_of(c * LANES, LANES), LANES)
        gate = jax.nn.sigmoid(dot3(parts(wgt[...]), parts(zhat[:, at] * gain0)))
        passed = load_cells(up, c, res) * gate
        d_out[:, at] = passed
        slope[:, at] = passed * (1.0 - gate)
        grad[:, at] = dot3(parts(w_out[...]), parts(passed)) * gain1
        return 0

    lax.fori_loop(0, up.shape[0] // LANES, step, 0)


def norm_back_kernel(n, got, grad, send, xhat):
    per = got.shape[0] // (9 * n)

    def step(c, _):
        at = pl.ds(pl.multiple_of(c * LANES, LANES), LANES)
        x = jnp.concatenate(
            [
                jnp.concatenate([got[tile_rows(n, per, 3 * c + t, q), :] for q in range(per)], axis=0)
                for t in range(3)
            ],
            axis=1,
        )
        normal, inverse = hat(x)
        xhat[:, at] = normal
        dx = hat_back(grad[:, at], normal, inverse)
        for q in range(per):
            for t in range(3):
                send[tile_rows(n, per, 3 * c + t, q), :] = dx[q * n : (q + 1) * n, t * 128 : (t + 1) * 128]
        return 0

    lax.fori_loop(0, xhat.shape[1] // LANES, step, 0)


def output_kernel(xhat, zhat, d_out, slope, w_gate, w_out, gains, dzn, mg, mo, wot):
    gain1 = column(gains[1:2, :])
    wot[...] = w_out[...].T
    mg[...] = jnp.zeros_like(mg)
    mo[...] = jnp.zeros_like(mo)

    def step(c, _):
        at = pl.ds(pl.multiple_of(c * LANES, LANES), LANES)
        normal = xhat[:, at]
        out = dot3(parts(wot[...]), parts(normal * gain1))
        d_logit = parts(slope[:, at] * out)
        mo[...] += dot3(parts(d_out[:, at]), parts(normal), NT)
        mg[...] += dot3(d_logit, parts(zhat[:, at]), NT)
        dzn[:, at] = dot3(parts(w_gate[...]), d_logit)
        return 0

    lax.fori_loop(0, xhat.shape[1] // LANES, step, 0)


def gather_dx(n, got, q, dx_all):
    per = got.shape[0] // (9 * n)
    for p in range(3):
        two = to_rows([got[tile_rows(n, per, 3 * p + t, q), :] for t in range(3)])
        for side in range(2):
            for half in range(2):
                dx_all[pl.ds((2 * p + side) * n, n), pl.ds(128 * half, 128)] = two[side][half]
    return parts(dx_all[...])


def b_back_kernel(n, res, got, swap, a_in, keep, give, dx_all, db_all):
    per = got.shape[0] // (9 * n)
    rows = res // (2 * n)
    pm = read_masks(swap, n, res)
    for q in range(per):
        db = dot3(gather_dx(n, got, q, dx_all), parts(a_in[q]), TN)
        db_all[0:256, :] = db[:, :128]
        db_all[256:512, :] = db[:, 128:]
        for p in range(rows // 2):
            tiles = []
            for core in range(2):
                two = []
                for row in (core * rows + 2 * p, core * rows + 2 * p + 1):
                    two.append(
                        [db_all[pl.ds(256 * half + row, n, stride=2 * rows), :] * pm[row][half] for half in range(2)]
                    )
                tiles.append(to_tiles(*two))
            for t in range(3):
                at = tile_rows(n, per, 3 * p + t, q)
                keep[at, :], give[at, :] = by_core(tiles[0][t], tiles[1][t])


def a_back_kernel(n, res, got, swap, b_in, send, dx_all):
    per = got.shape[0] // (9 * n)
    rows = res // (2 * n)
    pm = read_masks(swap, n, res)
    for q in range(per):
        base = 512 * q
        b_whole = jnp.concatenate([b_in[pl.ds(base, 256), :], b_in[pl.ds(base + 256, 256), :]], axis=1)
        da = dot3(gather_dx(n, got, q, dx_all), parts(b_whole))
        for p in range(rows // 2):
            two = []
            for il in (2 * p, 2 * p + 1):
                own = [by_core(pm[il][half], pm[rows + il][half])[0] for half in range(2)]
                two.append([da[il * n : (il + 1) * n, 128 * half : 128 * half + 128] * own[half] for half in range(2)])
            for t, tile in enumerate(to_tiles(*two)):
                send[tile_rows(n, 2 * per, 3 * p + t, q), :] = tile


def add_kernel(half_sent, keep, taken, send):
    per = keep.shape[1]
    send[:, :per, :] = half_sent[:, :per, :]
    send[:, per:, :] = keep[...] + taken[...]


def read_grads(n, got, val, sig, c, which):
    hidden = val.shape[0] // 2
    per = hidden // n
    at = pl.ds(pl.multiple_of(c * LANES, LANES), LANES)
    d = jnp.concatenate(
        [
            jnp.concatenate([got[tile_rows(n, 2 * per, 3 * c + t, which * per + q), :] for q in range(per)], axis=0)
            for t in range(3)
        ],
        axis=1,
    )
    rows = pl.ds(which * hidden, hidden)
    gate = sig[rows, at]
    d_val = d * gate
    return d_val, d_val * val[rows, at] * (1.0 - gate)


def weight_kernel(n, got, zhat, val, sig, mg, mo, keep, give, mi):
    hidden = val.shape[0] // 2
    mi[...] = jnp.zeros_like(mi)

    def step(c, _):
        at = pl.ds(pl.multiple_of(c * LANES, LANES), LANES)
        z = parts(zhat[:, at])
        for which in range(2):
            for k, grad in enumerate(read_grads(n, got, val, sig, c, which)):
                mi[pl.ds((2 * which + k) * hidden, hidden), :] += dot3(parts(grad), z, NT)
        return 0

    lax.fori_loop(0, zhat.shape[1] // LANES, step, 0)
    half = keep.shape[0]
    low = mi[pl.ds(0, half), :]
    high = jnp.concatenate([mi[pl.ds(half, mi.shape[0] - half), :], mg[...], mo[...]], axis=0)
    keep[...], give[...] = by_core(low, high)


def input_kernel(n, res, got, zhat, zinv, val, sig, dzn, w_in, gains, d_pair, w_hi, w_lo):
    hidden = val.shape[0] // 2
    wh, wl = parts(w_in[...])
    w_hi[...], w_lo[...] = wh, wl
    gain0 = column(gains[0:1, :])

    def step(c, _):
        at = pl.ds(pl.multiple_of(c * LANES, LANES), LANES)
        total = dzn[:, at]
        for which in range(2):
            for k, grad in enumerate(read_grads(n, got, val, sig, c, which)):
                cols = pl.ds((2 * which + k) * hidden, hidden)
                total += dot3((w_hi[:, cols], w_lo[:, cols]), parts(grad))
        store_cells(d_pair, c, res, hat_back(total * gain0, zhat[:, at], zinv[:, at]))
        return 0

    lax.fori_loop(0, d_pair.shape[0] // LANES, step, 0)


def finish_kernel(mine, theirs, w_in, w_gate, w_out, gains, d_w_in, d_w_gate, d_w_out, d_gains, m):
    width = w_out.shape[0]
    half = mine.shape[0]
    m[0:half, :], m[half:, :] = by_core(mine[...], theirs[...])
    gain0, gain1 = column(gains[0:1, :]), column(gains[1:2, :])
    fold = jnp.zeros((width, width), F32)
    for k in range(w_in.shape[1] // width):
        cols = pl.ds(k * width, width)
        part = m[cols, :].T
        d_w_in[:, cols] = part * gain0
        fold += part * w_in[:, cols]
    base = w_in.shape[1]
    part = m[pl.ds(base, width), :].T
    d_w_gate[...] = part * gain0
    fold += part * w_gate[...]
    d_gains[0:1, :] = jnp.sum(fold.T, axis=0, keepdims=True)
    part = m[pl.ds(base + width, width), :].T
    d_w_out[...] = part * gain1
    d_gains[1:2, :] = jnp.sum((part * w_out[...]).T, axis=0, keepdims=True)


def exchange(x, axis, groups):
    return lax.all_to_all(x, axis, 0, 0, tiled=True, axis_index_groups=groups)


def swap_cores(x, n):
    return lax.ppermute(x, "dap", [(i, i ^ 1) for i in range(2 * n)])


BOTH = ("dp", "dap")
NY = 4


def plane_and_line(n, n_dp):
    nx = max(1, n_dp // 2)
    nlo, nhi = n_dp // nx, n // NY

    def index(x, y, hi, lo, core):
        return (lo * nx + x) * 2 * n + (y * nhi + hi) * 2 + core

    planes = [
        [index(x, y, hi, lo, core) for x in range(nx) for y in range(NY)]
        for hi in range(nhi)
        for lo in range(nlo)
        for core in range(2)
    ]
    lines = [
        [index(x, y, hi, lo, core) for hi in range(nhi) for lo in range(nlo)]
        for x in range(nx)
        for y in range(NY)
        for core in range(2)
    ]
    return planes, lines


def reduce_all(keep, give, n, n_dp):
    planes, lines = plane_and_line(n, n_dp)
    count, width = keep.shape

    def summed(x, groups, pieces):
        return jnp.sum(exchange(x.reshape(pieces, -1, width), BOTH, groups), axis=0)

    def spread(x, pieces):
        return jnp.broadcast_to(x[None], (pieces,) + x.shape)

    in_plane, in_line = len(planes[0]), len(lines[0])
    mine = summed(keep + swap_cores(give, n), planes, in_plane)
    mine = summed(spread(mine, in_line), lines, in_line)
    return exchange(spread(mine, in_plane), BOTH, planes).reshape(count, width)


def shards(devices, n_dp, pair, upstream, residue_mask, w_in, w_gate, w_out, gains):
    _, rows, res, width = pair.shape
    hidden = w_out.shape[0]
    cells = rows * res
    n = devices // 2
    per = hidden // n
    same_core = [list(range(core, devices, 2)) for core in range(2)]
    pair2 = pair.reshape(cells, width)
    up2 = upstream.reshape(cells, width)
    tiles = n * 9 * per

    def wide(x):
        return exchange(x.reshape(n, 18 * per, 128), "dap", same_core).reshape(2 * tiles, 128)

    def narrow(x):
        return exchange(x.reshape(n, 9 * per, 128), "dap", same_core).reshape(tiles, 128)

    flat = (width, cells)
    product = 6 * width * hidden * cells

    send, zhat, zinv, val, sig = call(
        functools.partial(project_kernel, n, res),
        [((2 * tiles, 128), F32), (flat, F32), ((1, cells), F32), ((2 * hidden, cells), F32), ((2 * hidden, cells), F32)],
        [pltpu.VMEM((4 * hidden, width), BF16)] * 2,
    )(pair2, w_in, gains)
    got = wide(send)

    other = swap_cores(got.reshape(n * 9, 2, per, 128)[:, 1].reshape(tiles, 128), n)
    up2, _ = lax.optimization_barrier((up2, got))
    d_out, slope, grad = call(
        functools.partial(gate_kernel, res),
        [(flat, F32)] * 3,
        [pltpu.VMEM((width, width), F32)],
        flops=2 * product,
        moved=4 * cells * width * 5,
    )(up2, zhat, w_gate, w_out, gains)
    send, a_all, b_all, pm = call(
        functools.partial(triangle_kernel, n),
        [((tiles, 128), F32), ((per, res // 2, 256), F32), ((per * 512, 128), F32), ((512, 128), F32)],
        [pltpu.VMEM((8, 256), F32)],
    )(got, other, residue_mask)
    got = narrow(send)

    send, xhat = call(functools.partial(norm_back_kernel, n), [((tiles, 128), F32), (flat, F32)])(got, grad)
    got = narrow(send)

    keep, give = call(
        functools.partial(b_back_kernel, n, res),
        [((tiles, 128), F32)] * 2,
        [pltpu.VMEM((res // 2, 256), F32), pltpu.VMEM((512, 128), F32)],
    )(got, pm, a_all)
    give, got, xhat = lax.optimization_barrier((give, got, xhat))
    taken = swap_cores(give, n)
    (send,) = call(
        functools.partial(a_back_kernel, n, res),
        [((2 * tiles, 128), F32)],
        [pltpu.VMEM((res // 2, 256), F32)],
        flops=product,
        moved=4 * cells * width * 4,
    )(got, pm, b_all)
    dzn, mg, mo = call(
        output_kernel,
        [(flat, F32), ((width, width), F32), ((width, hidden), F32)],
        [pltpu.VMEM((width, hidden), F32)],
        flops=4 * product,
        moved=4 * cells * width * 5,
    )(xhat, zhat, d_out, slope, w_gate, w_out, gains)
    group = (n * 9, per, 128)
    (send,) = call(add_kernel, [((n * 9, 2 * per, 128), F32)])(
        send.reshape(n * 9, 2 * per, 128), keep.reshape(group), taken.reshape(group)
    )
    got = wide(send)

    half = (4 * hidden + 2 * width) // 2
    keep, give = call(
        functools.partial(weight_kernel, n),
        [((half, width), F32), ((half, width), F32)],
        [pltpu.VMEM((4 * hidden, width), F32)],
    )(got, zhat, val, sig, mg, mo)
    mine = reduce_all(keep, give, n, n_dp)
    mine, got = lax.optimization_barrier((mine, got))
    theirs = swap_cores(mine, n)
    (d_pair,) = call(
        functools.partial(input_kernel, n, res),
        [((cells, width), F32)],
        [pltpu.VMEM((width, 4 * hidden), BF16)] * 2,
        flops=4 * product,
        moved=4 * cells * width * 7,
    )(got, zhat, zinv, val, sig, dzn, w_in, gains)

    d_w_in, d_w_gate, d_w_out, d_gains = call(
        finish_kernel,
        [(w_in.shape, F32), (w_gate.shape, F32), (w_out.shape, F32), (gains.shape, F32)],
        [pltpu.VMEM((2 * half, width), F32)],
    )(mine, theirs, w_in, w_gate, w_out, gains)
    return (d_pair.reshape(pair.shape), d_w_in, d_w_gate, d_w_out, d_gains)


def solution(mesh):
    cells = P("dp", "dap", None, None)
    in_specs = (cells, cells, P("dp", None), P(), P(), P(), P())
    out_specs = (cells, P(), P(), P(), P())
    body = functools.partial(shards, mesh.shape["dap"], mesh.shape["dp"])
    return jax.shard_map(body, mesh=mesh, in_specs=in_specs, out_specs=out_specs, check_vma=False)
```

```python
import functools

import jax
import jax.numpy as jnp
from jax import lax
from jax.experimental import pallas as pl
from jax.experimental.pallas import tpu as pltpu
from jax.sharding import PartitionSpec as P

F32 = jnp.float32
BF16 = jnp.bfloat16
LANES = 384
EPS = 1e-05


def parts(x):
    hi = x.astype(BF16)
    return hi, (x - hi.astype(F32)).astype(BF16)


def dot3(left, right, dims=((1,), (0,))):
    (ah, al), (bh, bl) = left, right

    def one(a, b):
        return lax.dot_general(a, b, (dims, ((), ())), preferred_element_type=F32)

    return one(ah, bh) + (one(ah, bl) + one(al, bh))


NT = ((1,), (1,))
TN = ((0,), (0,))


def stack_left(x):
    hi, lo = parts(x)
    return jnp.concatenate(
        [jnp.concatenate([hi, hi], axis=1), jnp.concatenate([lo, jnp.zeros_like(lo)], axis=1)], axis=0
    )


def stack_rows(x):
    return jnp.concatenate(parts(x), axis=0)


def dot_stacked(left, right):
    both = jnp.dot(left, right, preferred_element_type=F32)
    m = left.shape[0] // 2
    return both[:m] + both[m:]


def dot_cells(left, right):
    both = lax.dot_general(left, right, (NT, ((), ())), preferred_element_type=F32)
    m, n = left.shape[0] // 2, right.shape[0] // 2
    return both[:m, :n] + both[:m, n:] + both[m:, :n]


def column(row):
    n = row.shape[1]
    return jnp.broadcast_to(row, (n, n)).T[:, :1]


def hat(x):
    center = x - jnp.mean(x, axis=0, keepdims=True)
    inverse = lax.rsqrt(jnp.mean(center * center, axis=0, keepdims=True) + EPS)
    return center * inverse, inverse


def hat_back(g, xhat, inverse):
    first = jnp.mean(g, axis=0, keepdims=True)
    second = jnp.mean(g * xhat, axis=0, keepdims=True)
    return inverse * (g - first - xhat * second)


def call(body, outs, scratch=(), flops=0, moved=0):
    return pl.pallas_call(
        body,
        out_shape=[jax.ShapeDtypeStruct(s, d) for s, d in outs],
        scratch_shapes=list(scratch),
        compiler_params=pltpu.CompilerParams(vmem_limit_bytes=16 * 2**20),
        cost_estimate=pl.CostEstimate(flops=flops, bytes_accessed=moved, transcendentals=0),
    )


def cell_slices(c, res):
    base = pl.multiple_of(c * 2 * res, 2 * res)
    return (
        pl.ds(base, 128),
        pl.ds(base + 128, res - 128),
        pl.ds(base + res + 128, res - 128),
        pl.ds(base + res, 128),
    )


def load_cells(ref, c, res):
    return jnp.concatenate([ref[at, :] for at in cell_slices(c, res)], axis=0).T


def store_cells(ref, c, res, value):
    value = value.T
    start = 0
    for at in cell_slices(c, res):
        ref[at, :] = value[start : start + at.size, :]
        start += at.size


def tile_rows(n, kinds, tile, kind):
    return pl.ds(tile * kinds + kind, n, stride=9 * kinds)


def to_rows(tiles):
    return (tiles[0], tiles[1]), (tiles[2], pltpu.roll(tiles[1], 64, 1))


def to_tiles(even, odd):
    low = lax.broadcasted_iota(jnp.int32, even[1].shape, 1) < 64
    return even[0], jnp.where(low, even[1], pltpu.roll(odd[1], 64, 1)), odd[0]


def project_kernel(n, res, pair, w_in, gains, send, zhat, zinv, val, sig, wt):
    hidden = w_in.shape[1] // 4
    per = hidden // n
    wh, wl = parts(w_in[...].T)
    wt[...] = jnp.concatenate([wh, wl, wh], axis=1)
    gain = column(gains[0:1, :])

    def step(c, _):
        at = pl.ds(pl.multiple_of(c * LANES, LANES), LANES)
        z, inverse = hat(load_cells(pair, c, res))
        zhat[:, at] = z
        zinv[:, at] = inverse
        zh, zl = parts(z * gain)
        zn = jnp.concatenate([zh, zh, zl], axis=0)
        for which in range(2):
            rows = pl.ds(2 * which * hidden, 2 * hidden)
            proj = jnp.dot(wt[rows, :], zn, preferred_element_type=F32)
            value, gate = proj[:hidden], jax.nn.sigmoid(proj[hidden:])
            val[pl.ds(which * hidden, hidden), at] = value
            sig[pl.ds(which * hidden, hidden), at] = gate
            both = value * gate
            for q in range(per):
                for t in range(3):
                    send[tile_rows(n, 2 * per, 3 * c + t, which * per + q), :] = both[
                        q * n : (q + 1) * n, t * 128 : (t + 1) * 128
                    ]
        return 0

    lax.fori_loop(0, pair.shape[0] // LANES, step, 0)


def make_masks(mask, line, swap):
    res = mask.shape[1]
    line[...] = jnp.zeros_like(line)
    line[0:1, pl.ds(0, res)] = mask[...].astype(F32)
    across = jnp.broadcast_to(line[0:1, :], (256, 256))
    both = across * across.T
    swap[0:256, :] = both[:, :128]
    swap[256:512, :] = both[:, 128:]


def read_masks(swap, n, res):
    rows = res // n
    return [[swap[pl.ds(256 * half + il, n, stride=rows), :] for half in range(2)] for il in range(rows)]


def core_of():
    return lax.rem(lax.axis_index("dap"), 2)


def by_core(mine, other):
    first = core_of() == 0
    return jnp.where(first, mine, other), jnp.where(first, other, mine)


def triangle_kernel(n, got, other, mask, send, a_out, b_out, swap, line):
    per = got.shape[0] // (2 * 9 * n)
    res = mask.shape[1]
    rows = res // (2 * n)
    make_masks(mask, line, swap)
    pm = read_masks(swap, n, res)
    for q in range(per):
        base = 512 * q
        for half in range(2):
            b_out[pl.ds(base + 256 * half + res, 256 - res), :] = jnp.zeros((256 - res, 128), F32)
        for p in range(rows // 2):
            two_a = to_rows([got[tile_rows(n, 2 * per, 3 * p + t, q), :] for t in range(3)])
            mine = [got[tile_rows(n, 2 * per, 3 * p + t, per + q), :] for t in range(3)]
            theirs = [other[tile_rows(n, per, 3 * p + t, q), :] for t in range(3)]
            tiles = [by_core(m, o) for m, o in zip(mine, theirs)]
            two_b = [to_rows([tile[core] for tile in tiles]) for core in range(2)]
            for side in range(2):
                il = 2 * p + side
                for half in range(2):
                    own = by_core(*[pm[core * rows + il][half] for core in range(2)])[0]
                    a_out[q, pl.ds(il * n, n), pl.ds(128 * half, 128)] = two_a[side][half] * own
                    for core in range(2):
                        row = core * rows + il
                        b_out[pl.ds(base + 256 * half + row, n, stride=2 * rows), :] = (
                            two_b[core][side][half] * pm[row][half]
                        )
        b_whole = jnp.concatenate([b_out[pl.ds(base, 256), :], b_out[pl.ds(base + 256, 256), :]], axis=1)
        x = dot3(parts(a_out[q]), parts(b_whole), NT)
        for p in range(rows // 2):
            even, odd = [
                [x[(2 * p + side) * n : (2 * p + side + 1) * n, 128 * half : 128 * half + 128] for half in range(2)]
                for side in range(2)
            ]
            for t, tile in enumerate(to_tiles(even, odd)):
                send[tile_rows(n, per, 3 * p + t, q), :] = tile


def gate_kernel(res, up, zhat, w_gate, w_out, gains, d_out, slope, grad, wgt, wo):
    gain0, gain1 = column(gains[0:1, :]), column(gains[1:2, :])
    wgt[...] = stack_left(w_gate[...].T)
    wo[...] = stack_left(w_out[...])

    def step(c, _):
        at = pl.ds(pl.multiple_of(c * LANES, LANES), LANES)
        gate = jax.nn.sigmoid(dot_stacked(wgt[...], stack_rows(zhat[:, at] * gain0)))
        passed = load_cells(up, c, res) * gate
        d_out[:, at] = passed
        slope[:, at] = passed * (1.0 - gate)
        grad[:, at] = dot_stacked(wo[...], stack_rows(passed)) * gain1
        return 0

    lax.fori_loop(0, up.shape[0] // LANES, step, 0)


def norm_back_kernel(n, got, grad, send, xhat):
    per = got.shape[0] // (9 * n)

    def step(c, _):
        at = pl.ds(pl.multiple_of(c * LANES, LANES), LANES)
        x = jnp.concatenate(
            [
                jnp.concatenate([got[tile_rows(n, per, 3 * c + t, q), :] for q in range(per)], axis=0)
                for t in range(3)
            ],
            axis=1,
        )
        normal, inverse = hat(x)
        xhat[:, at] = normal
        dx = hat_back(grad[:, at], normal, inverse)
        for q in range(per):
            for t in range(3):
                send[tile_rows(n, per, 3 * c + t, q), :] = dx[q * n : (q + 1) * n, t * 128 : (t + 1) * 128]
        return 0

    lax.fori_loop(0, xhat.shape[1] // LANES, step, 0)


def output_kernel(xhat, zhat, d_out, slope, w_gate, w_out, gains, dzn, mg, mo, wot, wg):
    gain1 = column(gains[1:2, :])
    wot[...] = stack_left(w_out[...].T)
    wg[...] = stack_left(w_gate[...])
    mg[...] = jnp.zeros_like(mg)
    mo[...] = jnp.zeros_like(mo)

    def step(c, _):
        at = pl.ds(pl.multiple_of(c * LANES, LANES), LANES)
        normal = xhat[:, at]
        d_logit = stack_rows(slope[:, at] * dot_stacked(wot[...], stack_rows(normal * gain1)))
        mo[...] += dot_cells(stack_rows(d_out[:, at]), stack_rows(normal))
        mg[...] += dot_cells(d_logit, stack_rows(zhat[:, at]))
        dzn[:, at] = dot_stacked(wg[...], d_logit)
        return 0

    lax.fori_loop(0, xhat.shape[1] // LANES, step, 0)


def gather_dx(n, got, q, dx_all):
    per = got.shape[0] // (9 * n)
    for p in range(3):
        two = to_rows([got[tile_rows(n, per, 3 * p + t, q), :] for t in range(3)])
        for side in range(2):
            for half in range(2):
                dx_all[pl.ds((2 * p + side) * n, n), pl.ds(128 * half, 128)] = two[side][half]
    return parts(dx_all[...])


def b_back_kernel(n, res, got, swap, a_in, keep, give, dx_all, db_all):
    per = got.shape[0] // (9 * n)
    rows = res // (2 * n)
    pm = read_masks(swap, n, res)
    for q in range(per):
        db = dot3(gather_dx(n, got, q, dx_all), parts(a_in[q]), TN)
        db_all[0:256, :] = db[:, :128]
        db_all[256:512, :] = db[:, 128:]
        for p in range(rows // 2):
            tiles = []
            for core in range(2):
                two = []
                for row in (core * rows + 2 * p, core * rows + 2 * p + 1):
                    two.append(
                        [db_all[pl.ds(256 * half + row, n, stride=2 * rows), :] * pm[row][half] for half in range(2)]
                    )
                tiles.append(to_tiles(*two))
            for t in range(3):
                at = tile_rows(n, per, 3 * p + t, q)
                keep[at, :], give[at, :] = by_core(tiles[0][t], tiles[1][t])


def a_back_kernel(n, res, got, swap, b_in, send, dx_all):
    per = got.shape[0] // (9 * n)
    rows = res // (2 * n)
    pm = read_masks(swap, n, res)
    for q in range(per):
        base = 512 * q
        b_whole = jnp.concatenate([b_in[pl.ds(base, 256), :], b_in[pl.ds(base + 256, 256), :]], axis=1)
        da = dot3(gather_dx(n, got, q, dx_all), parts(b_whole))
        for p in range(rows // 2):
            two = []
            for il in (2 * p, 2 * p + 1):
                own = [by_core(pm[il][half], pm[rows + il][half])[0] for half in range(2)]
                two.append([da[il * n : (il + 1) * n, 128 * half : 128 * half + 128] * own[half] for half in range(2)])
            for t, tile in enumerate(to_tiles(*two)):
                send[tile_rows(n, 2 * per, 3 * p + t, q), :] = tile


def add_kernel(half_sent, keep, taken, send):
    per = keep.shape[1]
    send[:, :per, :] = half_sent[:, :per, :]
    send[:, per:, :] = keep[...] + taken[...]


def read_grads(n, got, val, sig, c, which):
    hidden = val.shape[0] // 2
    per = hidden // n
    at = pl.ds(pl.multiple_of(c * LANES, LANES), LANES)
    d = jnp.concatenate(
        [
            jnp.concatenate([got[tile_rows(n, 2 * per, 3 * c + t, which * per + q), :] for q in range(per)], axis=0)
            for t in range(3)
        ],
        axis=1,
    )
    rows = pl.ds(which * hidden, hidden)
    gate = sig[rows, at]
    d_val = d * gate
    return d_val, d_val * val[rows, at] * (1.0 - gate)


def input_kernel(n, res, got, zhat, zinv, val, sig, dzn, w_in, gains, mg, mo, d_pair, keep, give, mi, w_two):
    width = zhat.shape[0]
    w_two[...] = stack_rows(w_in[...])
    gain0 = column(gains[0:1, :])
    mi[...] = jnp.zeros_like(mi)

    def step(c, _):
        at = pl.ds(pl.multiple_of(c * LANES, LANES), LANES)
        z = zhat[:, at]
        grads = [grad for which in range(2) for grad in read_grads(n, got, val, sig, c, which)]
        hi, lo = parts(jnp.concatenate(grads, axis=0))
        mi[...] += dot_cells(jnp.concatenate([hi, lo], axis=0), stack_rows(z))
        both = jnp.dot(w_two[...], hi, preferred_element_type=F32)
        total = both[:width] + both[width:] + jnp.dot(w_two[:width, :], lo, preferred_element_type=F32)
        store_cells(d_pair, c, res, hat_back((total + dzn[:, at]) * gain0, z, zinv[:, at]))
        return 0

    lax.fori_loop(0, zhat.shape[1] // LANES, step, 0)
    half = keep.shape[0]
    low = mi[pl.ds(0, half), :]
    high = jnp.concatenate([mi[pl.ds(half, mi.shape[0] - half), :], mg[...], mo[...]], axis=0)
    keep[...], give[...] = by_core(low, high)


def finish_kernel(mine, theirs, w_in, w_gate, w_out, gains, d_w_in, d_w_gate, d_w_out, d_gains, m):
    width = w_out.shape[0]
    half = mine.shape[0]
    m[0:half, :], m[half:, :] = by_core(mine[...], theirs[...])
    gain0, gain1 = column(gains[0:1, :]), column(gains[1:2, :])
    fold = jnp.zeros((width, width), F32)
    for k in range(w_in.shape[1] // width):
        cols = pl.ds(k * width, width)
        part = m[cols, :].T
        d_w_in[:, cols] = part * gain0
        fold += part * w_in[:, cols]
    base = w_in.shape[1]
    part = m[pl.ds(base, width), :].T
    d_w_gate[...] = part * gain0
    fold += part * w_gate[...]
    d_gains[0:1, :] = jnp.sum(fold.T, axis=0, keepdims=True)
    part = m[pl.ds(base + width, width), :].T
    d_w_out[...] = part * gain1
    d_gains[1:2, :] = jnp.sum((part * w_out[...]).T, axis=0, keepdims=True)


def exchange(x, axis, groups):
    return lax.all_to_all(x, axis, 0, 0, tiled=True, axis_index_groups=groups)


def swap_cores(x, n):
    return lax.ppermute(x, "dap", [(i, i ^ 1) for i in range(2 * n)])


BOTH = ("dp", "dap")
NY = 4


def plane_and_line(n, n_dp):
    nx = max(1, n_dp // 2)
    nlo, nhi = n_dp // nx, n // NY

    def index(x, y, hi, lo, core):
        return (lo * nx + x) * 2 * n + (y * nhi + hi) * 2 + core

    planes = [
        [index(x, y, hi, lo, core) for x in range(nx) for y in range(NY)]
        for hi in range(nhi)
        for lo in range(nlo)
        for core in range(2)
    ]
    lines = [
        [index(x, y, hi, lo, core) for hi in range(nhi) for lo in range(nlo)]
        for x in range(nx)
        for y in range(NY)
        for core in range(2)
    ]
    return planes, lines


def reduce_all(keep, give, n, n_dp):
    planes, lines = plane_and_line(n, n_dp)
    count, width = keep.shape

    def summed(x, groups, pieces):
        return jnp.sum(exchange(x.reshape(pieces, -1, width), BOTH, groups), axis=0)

    def spread(x, pieces):
        return jnp.broadcast_to(x[None], (pieces,) + x.shape)

    in_plane, in_line = len(planes[0]), len(lines[0])
    mine = summed(keep + swap_cores(give, n), planes, in_plane)
    mine = summed(spread(mine, in_line), lines, in_line)
    return exchange(spread(mine, in_plane), BOTH, planes).reshape(count, width)


def shards(devices, n_dp, pair, upstream, residue_mask, w_in, w_gate, w_out, gains):
    _, rows, res, width = pair.shape
    hidden = w_out.shape[0]
    cells = rows * res
    n = devices // 2
    per = hidden // n
    same_core = [list(range(core, devices, 2)) for core in range(2)]
    pair2 = pair.reshape(cells, width)
    up2 = upstream.reshape(cells, width)
    tiles = n * 9 * per

    def wide(x):
        return exchange(x.reshape(n, 18 * per, 128), "dap", same_core).reshape(2 * tiles, 128)

    def narrow(x):
        return exchange(x.reshape(n, 9 * per, 128), "dap", same_core).reshape(tiles, 128)

    flat = (width, cells)
    product = 6 * width * hidden * cells

    send, zhat, zinv, val, sig = call(
        functools.partial(project_kernel, n, res),
        [((2 * tiles, 128), F32), (flat, F32), ((1, cells), F32), ((2 * hidden, cells), F32), ((2 * hidden, cells), F32)],
        [pltpu.VMEM((4 * hidden, 3 * width), BF16)],
    )(pair2, w_in, gains)
    got = wide(send)

    other = swap_cores(got.reshape(n * 9, 2, per, 128)[:, 1].reshape(tiles, 128), n)
    up2, _ = lax.optimization_barrier((up2, got))
    d_out, slope, grad = call(
        functools.partial(gate_kernel, res),
        [(flat, F32)] * 3,
        [pltpu.VMEM((2 * width, 2 * width), BF16), pltpu.VMEM((2 * hidden, 2 * width), BF16)],
        flops=2 * product,
        moved=4 * cells * width * 5,
    )(up2, zhat, w_gate, w_out, gains)
    other, d_out = lax.optimization_barrier((other, d_out))
    send, a_all, b_all, pm = call(
        functools.partial(triangle_kernel, n),
        [((tiles, 128), F32), ((per, res // 2, 256), F32), ((per * 512, 128), F32), ((512, 128), F32)],
        [pltpu.VMEM((8, 256), F32)],
    )(got, other, residue_mask)
    got = narrow(send)

    send, xhat = call(functools.partial(norm_back_kernel, n), [((tiles, 128), F32), (flat, F32)])(got, grad)
    got = narrow(send)

    keep, give = call(
        functools.partial(b_back_kernel, n, res),
        [((tiles, 128), F32)] * 2,
        [pltpu.VMEM((res // 2, 256), F32), pltpu.VMEM((512, 128), F32)],
    )(got, pm, a_all)
    give, got, xhat = lax.optimization_barrier((give, got, xhat))
    taken = swap_cores(give, n)
    (send,) = call(
        functools.partial(a_back_kernel, n, res),
        [((2 * tiles, 128), F32)],
        [pltpu.VMEM((res // 2, 256), F32)],
        flops=product,
        moved=4 * cells * width * 4,
    )(got, pm, b_all)
    dzn, mg, mo = call(
        output_kernel,
        [(flat, F32), ((width, width), F32), ((width, hidden), F32)],
        [pltpu.VMEM((2 * width, 2 * hidden), BF16), pltpu.VMEM((2 * width, 2 * width), BF16)],
        flops=4 * product,
        moved=4 * cells * width * 5,
    )(xhat, zhat, d_out, slope, w_gate, w_out, gains)
    taken, dzn, send = lax.optimization_barrier((taken, dzn, send))
    group = (n * 9, per, 128)
    (send,) = call(add_kernel, [((n * 9, 2 * per, 128), F32)])(
        send.reshape(n * 9, 2 * per, 128), keep.reshape(group), taken.reshape(group)
    )
    got = wide(send)

    half = (4 * hidden + 2 * width) // 2
    d_pair, keep, give = call(
        functools.partial(input_kernel, n, res),
        [((cells, width), F32), ((half, width), F32), ((half, width), F32)],
        [pltpu.VMEM((4 * hidden, width), F32), pltpu.VMEM((2 * width, 4 * hidden), BF16)],
    )(got, zhat, zinv, val, sig, dzn, w_in, gains, mg, mo)
    mine = reduce_all(keep, give, n, n_dp)
    theirs = swap_cores(mine, n)

    d_w_in, d_w_gate, d_w_out, d_gains = call(
        finish_kernel,
        [(w_in.shape, F32), (w_gate.shape, F32), (w_out.shape, F32), (gains.shape, F32)],
        [pltpu.VMEM((2 * half, width), F32)],
    )(mine, theirs, w_in, w_gate, w_out, gains)
    return (d_pair.reshape(pair.shape), d_w_in, d_w_gate, d_w_out, d_gains)


def solution(mesh):
    cells = P("dp", "dap", None, None)
    in_specs = (cells, cells, P("dp", None), P(), P(), P(), P())
    out_specs = (cells, P(), P(), P(), P())
    body = functools.partial(shards, mesh.shape["dap"], mesh.shape["dp"])
    return jax.shard_map(body, mesh=mesh, in_specs=in_specs, out_specs=out_specs, check_vma=False)
```

```python
import functools

import jax
import jax.numpy as jnp
from jax import lax
from jax.experimental import pallas as pl
from jax.experimental.pallas import tpu as pltpu
from jax.sharding import PartitionSpec as P

F32 = jnp.float32
BF16 = jnp.bfloat16
LANES = 384
EPS = 1e-05


def parts(x):
    hi = x.astype(BF16)
    return hi, (x - hi.astype(F32)).astype(BF16)


def dot3(left, right, dims=((1,), (0,))):
    (ah, al), (bh, bl) = left, right

    def one(a, b):
        return lax.dot_general(a, b, (dims, ((), ())), preferred_element_type=F32)

    if dims == TN:
        return one(jnp.concatenate([ah, al], axis=0), jnp.concatenate([bh, bh], axis=0)) + one(ah, bl)
    both = one(jnp.concatenate([ah, al], axis=0), bh)
    m = ah.shape[0]
    return both[:m] + (both[m:] + one(ah, bl))


NT = ((1,), (1,))
TN = ((0,), (0,))


def stack_left(x):
    hi, lo = parts(x)
    return jnp.concatenate(
        [jnp.concatenate([hi, hi], axis=1), jnp.concatenate([lo, jnp.zeros_like(lo)], axis=1)], axis=0
    )


def stack_rows(x):
    return jnp.concatenate(parts(x), axis=0)


def dot_stacked(left, right):
    both = jnp.dot(left, right, preferred_element_type=F32)
    m = left.shape[0] // 2
    return both[:m] + both[m:]


def dot_cells(left, right):
    both = lax.dot_general(left, right, (NT, ((), ())), preferred_element_type=F32)
    m, n = left.shape[0] // 2, right.shape[0] // 2
    return both[:m, :n] + both[:m, n:] + both[m:, :n]


def column(row):
    n = row.shape[1]
    return jnp.broadcast_to(row, (n, n)).T[:, :1]


def hat(x):
    center = x - jnp.mean(x, axis=0, keepdims=True)
    inverse = lax.rsqrt(jnp.mean(center * center, axis=0, keepdims=True) + EPS)
    return center * inverse, inverse


def hat_back(g, xhat, inverse):
    first = jnp.mean(g, axis=0, keepdims=True)
    second = jnp.mean(g * xhat, axis=0, keepdims=True)
    return inverse * (g - first - xhat * second)


def call(body, outs, scratch=(), flops=0, moved=0):
    return pl.pallas_call(
        body,
        out_shape=[jax.ShapeDtypeStruct(s, d) for s, d in outs],
        scratch_shapes=list(scratch),
        compiler_params=pltpu.CompilerParams(vmem_limit_bytes=16 * 2**20),
        cost_estimate=pl.CostEstimate(flops=flops, bytes_accessed=moved, transcendentals=0),
    )


def cell_slices(c, res):
    base = pl.multiple_of(c * 2 * res, 2 * res)
    return (
        pl.ds(base, 128),
        pl.ds(base + 128, res - 128),
        pl.ds(base + res + 128, res - 128),
        pl.ds(base + res, 128),
    )


def load_cells(ref, c, res):
    return jnp.concatenate([ref[at, :] for at in cell_slices(c, res)], axis=0).T


def store_cells(ref, c, res, value):
    value = value.T
    start = 0
    for at in cell_slices(c, res):
        ref[at, :] = value[start : start + at.size, :]
        start += at.size


def tile_rows(n, kinds, tile, kind):
    return pl.ds(tile * kinds + kind, n, stride=9 * kinds)


def to_rows(tiles):
    return (tiles[0], tiles[1]), (tiles[2], pltpu.roll(tiles[1], 64, 1))


def to_tiles(even, odd):
    low = lax.broadcasted_iota(jnp.int32, even[1].shape, 1) < 64
    return even[0], jnp.where(low, even[1], pltpu.roll(odd[1], 64, 1)), odd[0]


def project_kernel(n, res, pair, w_in, gains, send, zhat, zinv, val, sig, wt):
    hidden = w_in.shape[1] // 4
    per = hidden // n
    wh, wl = parts(w_in[...].T)
    wt[...] = jnp.concatenate([wh, wl, wh], axis=1)
    gain = column(gains[0:1, :])

    def step(c, _):
        at = pl.ds(pl.multiple_of(c * LANES, LANES), LANES)
        z, inverse = hat(load_cells(pair, c, res))
        zhat[:, at] = z
        zinv[:, at] = inverse
        zh, zl = parts(z * gain)
        zn = jnp.concatenate([zh, zh, zl], axis=0)
        for which in range(2):
            rows = pl.ds(2 * which * hidden, 2 * hidden)
            proj = jnp.dot(wt[rows, :], zn, preferred_element_type=F32)
            value, gate = proj[:hidden], jax.nn.sigmoid(proj[hidden:])
            val[pl.ds(which * hidden, hidden), at] = value
            sig[pl.ds(which * hidden, hidden), at] = gate
            both = value * gate
            for q in range(per):
                for t in range(3):
                    send[tile_rows(n, 2 * per, 3 * c + t, which * per + q), :] = both[
                        q * n : (q + 1) * n, t * 128 : (t + 1) * 128
                    ]
        return 0

    lax.fori_loop(0, pair.shape[0] // LANES, step, 0)


def make_masks(mask, line, swap):
    res = mask.shape[1]
    line[...] = jnp.zeros_like(line)
    line[0:1, pl.ds(0, res)] = mask[...].astype(F32)
    across = jnp.broadcast_to(line[0:1, :], (256, 256))
    both = across * across.T
    swap[0:256, :] = both[:, :128]
    swap[256:512, :] = both[:, 128:]


def read_masks(swap, n, res):
    rows = res // n
    return [[swap[pl.ds(256 * half + il, n, stride=rows), :] for half in range(2)] for il in range(rows)]


def core_of():
    return lax.rem(lax.axis_index("dap"), 2)


def by_core(mine, other):
    first = core_of() == 0
    return jnp.where(first, mine, other), jnp.where(first, other, mine)


def triangle_kernel(n, got, other, mask, send, a_out, b_out, swap, line):
    per = got.shape[0] // (2 * 9 * n)
    res = mask.shape[1]
    rows = res // (2 * n)
    make_masks(mask, line, swap)
    pm = read_masks(swap, n, res)
    for q in range(per):
        base = 512 * q
        for half in range(2):
            b_out[pl.ds(base + 256 * half + res, 256 - res), :] = jnp.zeros((256 - res, 128), F32)
        for p in range(rows // 2):
            two_a = to_rows([got[tile_rows(n, 2 * per, 3 * p + t, q), :] for t in range(3)])
            mine = [got[tile_rows(n, 2 * per, 3 * p + t, per + q), :] for t in range(3)]
            theirs = [other[tile_rows(n, per, 3 * p + t, q), :] for t in range(3)]
            tiles = [by_core(m, o) for m, o in zip(mine, theirs)]
            two_b = [to_rows([tile[core] for tile in tiles]) for core in range(2)]
            for side in range(2):
                il = 2 * p + side
                for half in range(2):
                    own = by_core(*[pm[core * rows + il][half] for core in range(2)])[0]
                    a_out[q, pl.ds(il * n, n), pl.ds(128 * half, 128)] = two_a[side][half] * own
                    for core in range(2):
                        row = core * rows + il
                        b_out[pl.ds(base + 256 * half + row, n, stride=2 * rows), :] = (
                            two_b[core][side][half] * pm[row][half]
                        )
        b_whole = jnp.concatenate([b_out[pl.ds(base, 256), :], b_out[pl.ds(base + 256, 256), :]], axis=1)
        x = dot3(parts(a_out[q]), parts(b_whole), NT)
        for p in range(rows // 2):
            even, odd = [
                [x[(2 * p + side) * n : (2 * p + side + 1) * n, 128 * half : 128 * half + 128] for half in range(2)]
                for side in range(2)
            ]
            for t, tile in enumerate(to_tiles(even, odd)):
                send[tile_rows(n, per, 3 * p + t, q), :] = tile


def gate_kernel(res, up, zhat, w_gate, w_out, gains, d_out, slope, grad, wgt, wo):
    gain0, gain1 = column(gains[0:1, :]), column(gains[1:2, :])
    wgt[...] = stack_left(w_gate[...].T)
    wo[...] = stack_left(w_out[...])

    def step(c, _):
        at = pl.ds(pl.multiple_of(c * LANES, LANES), LANES)
        gate = jax.nn.sigmoid(dot_stacked(wgt[...], stack_rows(zhat[:, at] * gain0)))
        passed = load_cells(up, c, res) * gate
        d_out[:, at] = passed
        slope[:, at] = passed * (1.0 - gate)
        grad[:, at] = dot_stacked(wo[...], stack_rows(passed)) * gain1
        return 0

    lax.fori_loop(0, up.shape[0] // LANES, step, 0)


def norm_back_kernel(n, got, grad, send, xhat):
    per = got.shape[0] // (9 * n)

    def step(c, _):
        at = pl.ds(pl.multiple_of(c * LANES, LANES), LANES)
        x = jnp.concatenate(
            [
                jnp.concatenate([got[tile_rows(n, per, 3 * c + t, q), :] for q in range(per)], axis=0)
                for t in range(3)
            ],
            axis=1,
        )
        normal, inverse = hat(x)
        xhat[:, at] = normal
        dx = hat_back(grad[:, at], normal, inverse)
        for q in range(per):
            for t in range(3):
                send[tile_rows(n, per, 3 * c + t, q), :] = dx[q * n : (q + 1) * n, t * 128 : (t + 1) * 128]
        return 0

    lax.fori_loop(0, xhat.shape[1] // LANES, step, 0)


def output_kernel(xhat, zhat, d_out, slope, w_gate, w_out, gains, dzn, mg, mo, wot, wg):
    gain1 = column(gains[1:2, :])
    wot[...] = stack_left(w_out[...].T)
    wg[...] = stack_left(w_gate[...])
    mg[...] = jnp.zeros_like(mg)
    mo[...] = jnp.zeros_like(mo)

    def step(c, _):
        at = pl.ds(pl.multiple_of(c * LANES, LANES), LANES)
        normal = xhat[:, at]
        d_logit = stack_rows(slope[:, at] * dot_stacked(wot[...], stack_rows(normal * gain1)))
        mo[...] += dot_cells(stack_rows(d_out[:, at]), stack_rows(normal))
        mg[...] += dot_cells(d_logit, stack_rows(zhat[:, at]))
        dzn[:, at] = dot_stacked(wg[...], d_logit)
        return 0

    lax.fori_loop(0, xhat.shape[1] // LANES, step, 0)


def gather_dx(n, got, q, dx_all):
    per = got.shape[0] // (9 * n)
    for p in range(3):
        two = to_rows([got[tile_rows(n, per, 3 * p + t, q), :] for t in range(3)])
        for side in range(2):
            for half in range(2):
                dx_all[pl.ds((2 * p + side) * n, n), pl.ds(128 * half, 128)] = two[side][half]
    return parts(dx_all[...])


def b_back_kernel(n, res, got, swap, a_in, keep, give, dx_all, db_all):
    per = got.shape[0] // (9 * n)
    rows = res // (2 * n)
    pm = read_masks(swap, n, res)
    for q in range(per):
        db = dot3(gather_dx(n, got, q, dx_all), parts(a_in[q]), TN)
        db_all[0:256, :] = db[:, :128]
        db_all[256:512, :] = db[:, 128:]
        for p in range(rows // 2):
            tiles = []
            for core in range(2):
                two = []
                for row in (core * rows + 2 * p, core * rows + 2 * p + 1):
                    two.append(
                        [db_all[pl.ds(256 * half + row, n, stride=2 * rows), :] * pm[row][half] for half in range(2)]
                    )
                tiles.append(to_tiles(*two))
            for t in range(3):
                at = tile_rows(n, per, 3 * p + t, q)
                keep[at, :], give[at, :] = by_core(tiles[0][t], tiles[1][t])


def a_back_kernel(n, res, got, swap, b_in, send, dx_all):
    per = got.shape[0] // (9 * n)
    rows = res // (2 * n)
    pm = read_masks(swap, n, res)
    for q in range(per):
        base = 512 * q
        b_whole = jnp.concatenate([b_in[pl.ds(base, 256), :], b_in[pl.ds(base + 256, 256), :]], axis=1)
        da = dot3(gather_dx(n, got, q, dx_all), parts(b_whole))
        for p in range(rows // 2):
            two = []
            for il in (2 * p, 2 * p + 1):
                own = [by_core(pm[il][half], pm[rows + il][half])[0] for half in range(2)]
                two.append([da[il * n : (il + 1) * n, 128 * half : 128 * half + 128] * own[half] for half in range(2)])
            for t, tile in enumerate(to_tiles(*two)):
                send[tile_rows(n, 2 * per, 3 * p + t, q), :] = tile


def add_kernel(half_sent, keep, taken, send):
    per = keep.shape[1]
    send[:, :per, :] = half_sent[:, :per, :]
    send[:, per:, :] = keep[...] + taken[...]


def read_grads(n, got, val, sig, c, which):
    hidden = val.shape[0] // 2
    per = hidden // n
    at = pl.ds(pl.multiple_of(c * LANES, LANES), LANES)
    d = jnp.concatenate(
        [
            jnp.concatenate([got[tile_rows(n, 2 * per, 3 * c + t, which * per + q), :] for q in range(per)], axis=0)
            for t in range(3)
        ],
        axis=1,
    )
    rows = pl.ds(which * hidden, hidden)
    gate = sig[rows, at]
    d_val = d * gate
    return d_val, d_val * val[rows, at] * (1.0 - gate)


def weight_kernel(n, got, zhat, val, sig, mg, mo, keep, give, d_hi, d_lo, mi):
    mi[...] = jnp.zeros_like(mi)

    def step(c, _):
        at = pl.ds(pl.multiple_of(c * LANES, LANES), LANES)
        grads = [grad for which in range(2) for grad in read_grads(n, got, val, sig, c, which)]
        hi, lo = parts(jnp.concatenate(grads, axis=0))
        d_hi[:, at], d_lo[:, at] = hi, lo
        mi[...] += dot_cells(jnp.concatenate([hi, lo], axis=0), stack_rows(zhat[:, at]))
        return 0

    lax.fori_loop(0, zhat.shape[1] // LANES, step, 0)
    half = keep.shape[0]
    low = mi[pl.ds(0, half), :]
    high = jnp.concatenate([mi[pl.ds(half, mi.shape[0] - half), :], mg[...], mo[...]], axis=0)
    keep[...], give[...] = by_core(low, high)


def input_kernel(res, d_hi, d_lo, zhat, zinv, dzn, w_in, gains, d_pair, w_two):
    width = zhat.shape[0]
    w_two[...] = stack_rows(w_in[...])
    gain0 = column(gains[0:1, :])

    def step(c, _):
        at = pl.ds(pl.multiple_of(c * LANES, LANES), LANES)
        both = jnp.dot(w_two[...], d_hi[:, at], preferred_element_type=F32)
        total = both[:width] + both[width:] + jnp.dot(w_two[:width, :], d_lo[:, at], preferred_element_type=F32)
        store_cells(d_pair, c, res, hat_back((total + dzn[:, at]) * gain0, zhat[:, at], zinv[:, at]))
        return 0

    lax.fori_loop(0, zhat.shape[1] // LANES, step, 0)


def finish_kernel(mine, theirs, w_in, w_gate, w_out, gains, d_w_in, d_w_gate, d_w_out, d_gains, m):
    width = w_out.shape[0]
    half = mine.shape[0]
    m[0:half, :], m[half:, :] = by_core(mine[...], theirs[...])
    gain0, gain1 = column(gains[0:1, :]), column(gains[1:2, :])
    fold = jnp.zeros((width, width), F32)
    for k in range(w_in.shape[1] // width):
        cols = pl.ds(k * width, width)
        part = m[cols, :].T
        d_w_in[:, cols] = part * gain0
        fold += part * w_in[:, cols]
    base = w_in.shape[1]
    part = m[pl.ds(base, width), :].T
    d_w_gate[...] = part * gain0
    fold += part * w_gate[...]
    d_gains[0:1, :] = jnp.sum(fold.T, axis=0, keepdims=True)
    part = m[pl.ds(base + width, width), :].T
    d_w_out[...] = part * gain1
    d_gains[1:2, :] = jnp.sum((part * w_out[...]).T, axis=0, keepdims=True)


def exchange(x, axis, groups):
    return lax.all_to_all(x, axis, 0, 0, tiled=True, axis_index_groups=groups)


def swap_cores(x, n):
    return lax.ppermute(x, "dap", [(i, i ^ 1) for i in range(2 * n)])


BOTH = ("dp", "dap")
NY = 4


def plane_and_line(n, n_dp):
    nx = max(1, n_dp // 2)
    nlo, nhi = n_dp // nx, n // NY

    def index(x, y, hi, lo, core):
        return (lo * nx + x) * 2 * n + (y * nhi + hi) * 2 + core

    planes = [
        [index(x, y, hi, lo, core) for x in range(nx) for y in range(NY)]
        for hi in range(nhi)
        for lo in range(nlo)
        for core in range(2)
    ]
    lines = [
        [index(x, y, hi, lo, core) for hi in range(nhi) for lo in range(nlo)]
        for x in range(nx)
        for y in range(NY)
        for core in range(2)
    ]
    return planes, lines


def reduce_all(keep, n, n_dp):
    planes, lines = plane_and_line(n, n_dp)
    count, width = keep.shape

    def summed(x, groups, pieces):
        return jnp.sum(exchange(x.reshape(pieces, -1, width), BOTH, groups), axis=0)

    def spread(x, pieces):
        return jnp.broadcast_to(x[None], (pieces,) + x.shape)

    in_plane, in_line = len(planes[0]), len(lines[0])
    mine = summed(keep, planes, in_plane)
    mine = summed(spread(mine, in_line), lines, in_line)
    return exchange(spread(mine, in_plane), BOTH, planes).reshape(count, width)


def shards(devices, n_dp, pair, upstream, residue_mask, w_in, w_gate, w_out, gains):
    _, rows, res, width = pair.shape
    hidden = w_out.shape[0]
    cells = rows * res
    n = devices // 2
    per = hidden // n
    same_core = [list(range(core, devices, 2)) for core in range(2)]
    pair2 = pair.reshape(cells, width)
    up2 = upstream.reshape(cells, width)
    tiles = n * 9 * per

    def wide(x):
        return exchange(x.reshape(n, 18 * per, 128), "dap", same_core).reshape(2 * tiles, 128)

    def narrow(x):
        return exchange(x.reshape(n, 9 * per, 128), "dap", same_core).reshape(tiles, 128)

    flat = (width, cells)
    product = 6 * width * hidden * cells

    send, zhat, zinv, val, sig = call(
        functools.partial(project_kernel, n, res),
        [((2 * tiles, 128), F32), (flat, F32), ((1, cells), F32), ((2 * hidden, cells), F32), ((2 * hidden, cells), F32)],
        [pltpu.VMEM((4 * hidden, 3 * width), BF16)],
    )(pair2, w_in, gains)
    got = wide(send)

    other = swap_cores(got.reshape(n * 9, 2, per, 128)[:, 1].reshape(tiles, 128), n)
    up2, _ = lax.optimization_barrier((up2, got))
    d_out, slope, grad = call(
        functools.partial(gate_kernel, res),
        [(flat, F32)] * 3,
        [pltpu.VMEM((2 * width, 2 * width), BF16), pltpu.VMEM((2 * hidden, 2 * width), BF16)],
        flops=2 * product,
        moved=4 * cells * width * 5,
    )(up2, zhat, w_gate, w_out, gains)
    other, d_out = lax.optimization_barrier((other, d_out))
    send, a_all, b_all, pm = call(
        functools.partial(triangle_kernel, n),
        [((tiles, 128), F32), ((per, res // 2, 256), F32), ((per * 512, 128), F32), ((512, 128), F32)],
        [pltpu.VMEM((8, 256), F32)],
    )(got, other, residue_mask)
    got = narrow(send)

    send, xhat = call(functools.partial(norm_back_kernel, n), [((tiles, 128), F32), (flat, F32)])(got, grad)
    got = narrow(send)

    keep, give = call(
        functools.partial(b_back_kernel, n, res),
        [((tiles, 128), F32)] * 2,
        [pltpu.VMEM((res // 2, 256), F32), pltpu.VMEM((512, 128), F32)],
    )(got, pm, a_all)
    give, got, xhat = lax.optimization_barrier((give, got, xhat))
    taken = swap_cores(give, n)
    (send,) = call(
        functools.partial(a_back_kernel, n, res),
        [((2 * tiles, 128), F32)],
        [pltpu.VMEM((res // 2, 256), F32)],
        flops=product,
        moved=4 * cells * width * 4,
    )(got, pm, b_all)
    dzn, mg, mo = call(
        output_kernel,
        [(flat, F32), ((width, width), F32), ((width, hidden), F32)],
        [pltpu.VMEM((2 * width, 2 * hidden), BF16), pltpu.VMEM((2 * width, 2 * width), BF16)],
        flops=4 * product,
        moved=4 * cells * width * 5,
    )(xhat, zhat, d_out, slope, w_gate, w_out, gains)
    taken, dzn, send = lax.optimization_barrier((taken, dzn, send))
    group = (n * 9, per, 128)
    (send,) = call(add_kernel, [((n * 9, 2 * per, 128), F32)])(
        send.reshape(n * 9, 2 * per, 128), keep.reshape(group), taken.reshape(group)
    )
    got = wide(send)

    half = (4 * hidden + 2 * width) // 2
    keep, give, d_hi, d_lo = call(
        functools.partial(weight_kernel, n),
        [((half, width), F32)] * 2 + [((4 * hidden, cells), BF16)] * 2,
        [pltpu.VMEM((4 * hidden, width), F32)],
    )(got, zhat, val, sig, mg, mo)
    taken = swap_cores(give, n)
    (d_pair,) = call(
        functools.partial(input_kernel, res),
        [((cells, width), F32)],
        [pltpu.VMEM((2 * width, 4 * hidden), BF16)],
        flops=4 * product,
        moved=4 * cells * width * 7,
    )(d_hi, d_lo, zhat, zinv, dzn, w_in, gains)
    taken, d_pair = lax.optimization_barrier((taken, d_pair))
    mine = reduce_all(keep + taken, n, n_dp)
    theirs = swap_cores(mine, n)

    d_w_in, d_w_gate, d_w_out, d_gains = call(
        finish_kernel,
        [(w_in.shape, F32), (w_gate.shape, F32), (w_out.shape, F32), (gains.shape, F32)],
        [pltpu.VMEM((2 * half, width), F32)],
    )(mine, theirs, w_in, w_gate, w_out, gains)
    return (d_pair.reshape(pair.shape), d_w_in, d_w_gate, d_w_out, d_gains)


def solution(mesh):
    cells = P("dp", "dap", None, None)
    in_specs = (cells, cells, P("dp", None), P(), P(), P(), P())
    out_specs = (cells, P(), P(), P(), P())
    body = functools.partial(shards, mesh.shape["dap"], mesh.shape["dp"])
    return jax.shard_map(body, mesh=mesh, in_specs=in_specs, out_specs=out_specs, check_vma=False)
```

```python
import functools

import jax
import jax.numpy as jnp
from jax import lax
from jax.experimental import pallas as pl
from jax.experimental.pallas import tpu as pltpu
from jax.sharding import PartitionSpec as P

F32 = jnp.float32
BF16 = jnp.bfloat16
LANES = 384
EPS = 1e-05


def parts(x):
    hi = x.astype(BF16)
    return hi, (x - hi.astype(F32)).astype(BF16)


def dot3(left, right, dims=((1,), (0,))):
    (ah, al), (bh, bl) = left, right

    def one(a, b):
        return lax.dot_general(a, b, (dims, ((), ())), preferred_element_type=F32)

    if dims == TN:
        return one(jnp.concatenate([ah, al], axis=0), jnp.concatenate([bh, bh], axis=0)) + one(ah, bl)
    both = one(jnp.concatenate([ah, al], axis=0), bh)
    m = ah.shape[0]
    return both[:m] + (both[m:] + one(ah, bl))


NT = ((1,), (1,))
TN = ((0,), (0,))


def stack_left(x):
    hi, lo = parts(x)
    return jnp.concatenate(
        [jnp.concatenate([hi, hi], axis=1), jnp.concatenate([lo, jnp.zeros_like(lo)], axis=1)], axis=0
    )


def stack_rows(x):
    return jnp.concatenate(parts(x), axis=0)


def dot_stacked(left, right):
    both = jnp.dot(left, right, preferred_element_type=F32)
    m = left.shape[0] // 2
    return both[:m] + both[m:]


def dot_cells(left, right):
    both = lax.dot_general(left, right, (NT, ((), ())), preferred_element_type=F32)
    m, n = left.shape[0] // 2, right.shape[0] // 2
    return both[:m, :n] + both[:m, n:] + both[m:, :n]


def column(row):
    n = row.shape[1]
    return jnp.broadcast_to(row, (n, n)).T[:, :1]


def hat(x):
    center = x - jnp.mean(x, axis=0, keepdims=True)
    inverse = lax.rsqrt(jnp.mean(center * center, axis=0, keepdims=True) + EPS)
    return center * inverse, inverse


def hat_back(g, xhat, inverse):
    first = jnp.mean(g, axis=0, keepdims=True)
    second = jnp.mean(g * xhat, axis=0, keepdims=True)
    return inverse * (g - first - xhat * second)


def call(body, outs, scratch=(), flops=0, moved=0):
    return pl.pallas_call(
        body,
        out_shape=[jax.ShapeDtypeStruct(s, d) for s, d in outs],
        scratch_shapes=list(scratch),
        compiler_params=pltpu.CompilerParams(vmem_limit_bytes=16 * 2**20),
        cost_estimate=pl.CostEstimate(flops=flops, bytes_accessed=moved, transcendentals=0),
    )


def cell_slices(c, res):
    base = c * 2 * res
    return (
        pl.ds(base, 128),
        pl.ds(base + 128, res - 128),
        pl.ds(base + res + 128, res - 128),
        pl.ds(base + res, 128),
    )


def load_cells(ref, c, res):
    return jnp.concatenate([ref[at, :] for at in cell_slices(c, res)], axis=0).T


def store_cells(ref, c, res, value):
    value = value.T
    start = 0
    for at in cell_slices(c, res):
        ref[at, :] = value[start : start + at.size, :]
        start += at.size


def tile_rows(n, kinds, tile, kind):
    return pl.ds(tile * kinds + kind, n, stride=9 * kinds)


def to_rows(tiles):
    return (tiles[0], tiles[1]), (tiles[2], pltpu.roll(tiles[1], 64, 1))


def to_tiles(even, odd):
    low = lax.broadcasted_iota(jnp.int32, even[1].shape, 1) < 64
    return even[0], jnp.where(low, even[1], pltpu.roll(odd[1], 64, 1)), odd[0]


def project_kernel(n, res, pair, w_in, gains, send, zhat, zinv, val, sig, wt):
    hidden = w_in.shape[1] // 4
    per = hidden // n
    wh, wl = parts(w_in[...].T)
    wt[...] = jnp.concatenate([wh, wl, wh], axis=1)
    gain = column(gains[0:1, :])

    def step(c):
        at = pl.ds(c * LANES, LANES)
        z, inverse = hat(load_cells(pair, c, res))
        zhat[:, at] = z
        zinv[:, at] = inverse
        zh, zl = parts(z * gain)
        zn = jnp.concatenate([zh, zh, zl], axis=0)
        for which in range(2):
            rows = pl.ds(2 * which * hidden, 2 * hidden)
            proj = jnp.dot(wt[rows, :], zn, preferred_element_type=F32)
            value, gate = proj[:hidden], jax.nn.sigmoid(proj[hidden:])
            val[pl.ds(which * hidden, hidden), at] = value
            sig[pl.ds(which * hidden, hidden), at] = gate
            both = value * gate
            for q in range(per):
                for t in range(3):
                    send[tile_rows(n, 2 * per, 3 * c + t, which * per + q), :] = both[
                        q * n : (q + 1) * n, t * 128 : (t + 1) * 128
                    ]

    for c in range(pair.shape[0] // LANES):
        step(c)


def make_masks(mask, line, swap):
    res = mask.shape[1]
    line[...] = jnp.zeros_like(line)
    line[0:1, pl.ds(0, res)] = mask[...].astype(F32)
    across = jnp.broadcast_to(line[0:1, :], (256, 256))
    both = across * across.T
    swap[0:256, :] = both[:, :128]
    swap[256:512, :] = both[:, 128:]


def read_masks(swap, n, res):
    rows = res // n
    return [[swap[pl.ds(256 * half + il, n, stride=rows), :] for half in range(2)] for il in range(rows)]


def core_of():
    return lax.rem(lax.axis_index("dap"), 2)


def by_core(mine, other):
    first = core_of() == 0
    return jnp.where(first, mine, other), jnp.where(first, other, mine)


def triangle_kernel(n, got, other, mask, send, a_out, b_out, swap, line):
    per = got.shape[0] // (2 * 9 * n)
    res = mask.shape[1]
    rows = res // (2 * n)
    make_masks(mask, line, swap)
    pm = read_masks(swap, n, res)
    for q in range(per):
        base = 512 * q
        for half in range(2):
            b_out[pl.ds(base + 256 * half + res, 256 - res), :] = jnp.zeros((256 - res, 128), F32)
        for p in range(rows // 2):
            two_a = to_rows([got[tile_rows(n, 2 * per, 3 * p + t, q), :] for t in range(3)])
            mine = [got[tile_rows(n, 2 * per, 3 * p + t, per + q), :] for t in range(3)]
            theirs = [other[tile_rows(n, per, 3 * p + t, q), :] for t in range(3)]
            tiles = [by_core(m, o) for m, o in zip(mine, theirs)]
            two_b = [to_rows([tile[core] for tile in tiles]) for core in range(2)]
            for side in range(2):
                il = 2 * p + side
                for half in range(2):
                    own = by_core(*[pm[core * rows + il][half] for core in range(2)])[0]
                    a_out[q, pl.ds(il * n, n), pl.ds(128 * half, 128)] = two_a[side][half] * own
                    for core in range(2):
                        row = core * rows + il
                        b_out[pl.ds(base + 256 * half + row, n, stride=2 * rows), :] = (
                            two_b[core][side][half] * pm[row][half]
                        )
        b_whole = jnp.concatenate([b_out[pl.ds(base, 256), :], b_out[pl.ds(base + 256, 256), :]], axis=1)
        x = dot3(parts(a_out[q]), parts(b_whole), NT)
        for p in range(rows // 2):
            even, odd = [
                [x[(2 * p + side) * n : (2 * p + side + 1) * n, 128 * half : 128 * half + 128] for half in range(2)]
                for side in range(2)
            ]
            for t, tile in enumerate(to_tiles(even, odd)):
                send[tile_rows(n, per, 3 * p + t, q), :] = tile


def gate_kernel(res, up, zhat, w_gate, w_out, gains, d_out, slope, grad, wgt, wo):
    gain0, gain1 = column(gains[0:1, :]), column(gains[1:2, :])
    wgt[...] = stack_left(w_gate[...].T)
    wo[...] = stack_left(w_out[...])

    def step(c):
        at = pl.ds(c * LANES, LANES)
        gate = jax.nn.sigmoid(dot_stacked(wgt[...], stack_rows(zhat[:, at] * gain0)))
        passed = load_cells(up, c, res) * gate
        d_out[:, at] = passed
        slope[:, at] = passed * (1.0 - gate)
        grad[:, at] = dot_stacked(wo[...], stack_rows(passed)) * gain1

    for c in range(up.shape[0] // LANES):
        step(c)


def norm_back_kernel(n, got, grad, send, xhat):
    per = got.shape[0] // (9 * n)

    def step(c):
        at = pl.ds(c * LANES, LANES)
        x = jnp.concatenate(
            [
                jnp.concatenate([got[tile_rows(n, per, 3 * c + t, q), :] for q in range(per)], axis=0)
                for t in range(3)
            ],
            axis=1,
        )
        normal, inverse = hat(x)
        xhat[:, at] = normal
        dx = hat_back(grad[:, at], normal, inverse)
        for q in range(per):
            for t in range(3):
                send[tile_rows(n, per, 3 * c + t, q), :] = dx[q * n : (q + 1) * n, t * 128 : (t + 1) * 128]

    for c in range(xhat.shape[1] // LANES):
        step(c)


def output_kernel(xhat, zhat, d_out, slope, w_gate, w_out, gains, dzn, mg, mo, wot, wg):
    gain1 = column(gains[1:2, :])
    wot[...] = stack_left(w_out[...].T)
    wg[...] = stack_left(w_gate[...])
    mg[...] = jnp.zeros_like(mg)
    mo[...] = jnp.zeros_like(mo)

    def step(c):
        at = pl.ds(c * LANES, LANES)
        normal = xhat[:, at]
        d_logit = stack_rows(slope[:, at] * dot_stacked(wot[...], stack_rows(normal * gain1)))
        mo[...] += dot_cells(stack_rows(d_out[:, at]), stack_rows(normal))
        mg[...] += dot_cells(d_logit, stack_rows(zhat[:, at]))
        dzn[:, at] = dot_stacked(wg[...], d_logit)

    for c in range(xhat.shape[1] // LANES):
        step(c)


def gather_dx(n, got, q, dx_all):
    per = got.shape[0] // (9 * n)
    for p in range(3):
        two = to_rows([got[tile_rows(n, per, 3 * p + t, q), :] for t in range(3)])
        for side in range(2):
            for half in range(2):
                dx_all[pl.ds((2 * p + side) * n, n), pl.ds(128 * half, 128)] = two[side][half]
    return parts(dx_all[...])


def b_back_kernel(n, res, got, swap, a_in, keep, give, dx_all, db_all):
    per = got.shape[0] // (9 * n)
    rows = res // (2 * n)
    pm = read_masks(swap, n, res)
    for q in range(per):
        db = dot3(gather_dx(n, got, q, dx_all), parts(a_in[q]), TN)
        db_all[0:256, :] = db[:, :128]
        db_all[256:512, :] = db[:, 128:]
        for p in range(rows // 2):
            tiles = []
            for core in range(2):
                two = []
                for row in (core * rows + 2 * p, core * rows + 2 * p + 1):
                    two.append(
                        [db_all[pl.ds(256 * half + row, n, stride=2 * rows), :] * pm[row][half] for half in range(2)]
                    )
                tiles.append(to_tiles(*two))
            for t in range(3):
                at = tile_rows(n, per, 3 * p + t, q)
                keep[at, :], give[at, :] = by_core(tiles[0][t], tiles[1][t])


def a_back_kernel(n, res, got, swap, b_in, send, dx_all):
    per = got.shape[0] // (9 * n)
    rows = res // (2 * n)
    pm = read_masks(swap, n, res)
    for q in range(per):
        base = 512 * q
        b_whole = jnp.concatenate([b_in[pl.ds(base, 256), :], b_in[pl.ds(base + 256, 256), :]], axis=1)
        da = dot3(gather_dx(n, got, q, dx_all), parts(b_whole))
        for p in range(rows // 2):
            two = []
            for il in (2 * p, 2 * p + 1):
                own = [by_core(pm[il][half], pm[rows + il][half])[0] for half in range(2)]
                two.append([da[il * n : (il + 1) * n, 128 * half : 128 * half + 128] * own[half] for half in range(2)])
            for t, tile in enumerate(to_tiles(*two)):
                send[tile_rows(n, 2 * per, 3 * p + t, q), :] = tile


def add_kernel(half_sent, keep, taken, send):
    per = keep.shape[1]
    send[:, :per, :] = half_sent[:, :per, :]
    send[:, per:, :] = keep[...] + taken[...]


def read_grads(n, got, val, sig, c, which):
    hidden = val.shape[0] // 2
    per = hidden // n
    at = pl.ds(c * LANES, LANES)
    d = jnp.concatenate(
        [
            jnp.concatenate([got[tile_rows(n, 2 * per, 3 * c + t, which * per + q), :] for q in range(per)], axis=0)
            for t in range(3)
        ],
        axis=1,
    )
    rows = pl.ds(which * hidden, hidden)
    gate = sig[rows, at]
    d_val = d * gate
    return d_val, d_val * val[rows, at] * (1.0 - gate)


def weight_kernel(n, got, zhat, val, sig, mg, mo, keep, give, d_hi, d_lo, mi):
    mi[...] = jnp.zeros_like(mi)

    def step(c):
        at = pl.ds(c * LANES, LANES)
        grads = [grad for which in range(2) for grad in read_grads(n, got, val, sig, c, which)]
        hi, lo = parts(jnp.concatenate(grads, axis=0))
        d_hi[:, at], d_lo[:, at] = hi, lo
        mi[...] += dot_cells(jnp.concatenate([hi, lo], axis=0), stack_rows(zhat[:, at]))

    for c in range(zhat.shape[1] // LANES):
        step(c)
    half = keep.shape[0]
    low = mi[pl.ds(0, half), :]
    high = jnp.concatenate([mi[pl.ds(half, mi.shape[0] - half), :], mg[...], mo[...]], axis=0)
    keep[...], give[...] = by_core(low, high)


def input_kernel(res, d_hi, d_lo, zhat, zinv, dzn, w_in, gains, d_pair, w_two, rows, sems):
    width = zhat.shape[0]
    w_two[...] = stack_rows(w_in[...])
    gain0 = column(gains[0:1, :])
    copies = []
    for c in range(rows.shape[0] // LANES):
        at = pl.ds(c * LANES, LANES)
        both = jnp.dot(w_two[...], d_hi[:, at], preferred_element_type=F32)
        total = both[:width] + both[width:] + jnp.dot(w_two[:width, :], d_lo[:, at], preferred_element_type=F32)
        store_cells(rows, c, res, hat_back((total + dzn[:, at]) * gain0, zhat[:, at], zinv[:, at]))
        copies.append(pltpu.make_async_copy(rows.at[at, :], d_pair.at[at, :], sems.at[c]))
        copies[-1].start()
    for copy in copies:
        copy.wait()


def finish_kernel(mine, theirs, w_in, w_gate, w_out, gains, d_w_in, d_w_gate, d_w_out, d_gains, m):
    width = w_out.shape[0]
    half = mine.shape[0]
    m[0:half, :], m[half:, :] = by_core(mine[...], theirs[...])
    gain0, gain1 = column(gains[0:1, :]), column(gains[1:2, :])
    fold = jnp.zeros((width, width), F32)
    for k in range(w_in.shape[1] // width):
        cols = pl.ds(k * width, width)
        part = m[cols, :].T
        d_w_in[:, cols] = part * gain0
        fold += part * w_in[:, cols]
    base = w_in.shape[1]
    part = m[pl.ds(base, width), :].T
    d_w_gate[...] = part * gain0
    fold += part * w_gate[...]
    d_gains[0:1, :] = jnp.sum(fold.T, axis=0, keepdims=True)
    part = m[pl.ds(base + width, width), :].T
    d_w_out[...] = part * gain1
    d_gains[1:2, :] = jnp.sum((part * w_out[...]).T, axis=0, keepdims=True)


def input_call(res, cells):
    def run(*operands):
        width = operands[2].shape[0]
        return pl.pallas_call(
            functools.partial(input_kernel, res),
            out_shape=[jax.ShapeDtypeStruct((cells, width), F32)],
            out_specs=[pl.BlockSpec(memory_space=pl.ANY)],
            scratch_shapes=[
                pltpu.VMEM((2 * width, operands[0].shape[0]), BF16),
                pltpu.VMEM((cells, width), F32),
                pltpu.SemaphoreType.DMA((cells // LANES,)),
            ],
            compiler_params=pltpu.CompilerParams(vmem_limit_bytes=16 * 2**20),
            cost_estimate=pl.CostEstimate(
                flops=24 * cells * width * width, bytes_accessed=28 * cells * width, transcendentals=0
            ),
        )(*operands)

    return run


def exchange(x, axis, groups):
    return lax.all_to_all(x, axis, 0, 0, tiled=True, axis_index_groups=groups)


def swap_cores(x, n):
    return lax.ppermute(x, "dap", [(i, i ^ 1) for i in range(2 * n)])


BOTH = ("dp", "dap")
NY = 4


def plane_and_line(n, n_dp):
    nx = max(1, n_dp // 2)
    nlo, nhi = n_dp // nx, n // NY

    def index(x, y, hi, lo, core):
        return (lo * nx + x) * 2 * n + (y * nhi + hi) * 2 + core

    planes = [
        [index(x, y, hi, lo, core) for x in range(nx) for y in range(NY)]
        for hi in range(nhi)
        for lo in range(nlo)
        for core in range(2)
    ]
    lines = [
        [index(x, y, hi, lo, core) for hi in range(nhi) for lo in range(nlo)]
        for x in range(nx)
        for y in range(NY)
        for core in range(2)
    ]
    return planes, lines


def reduce_all(keep, n, n_dp):
    planes, lines = plane_and_line(n, n_dp)
    count, width = keep.shape

    def summed(x, groups, pieces):
        return jnp.sum(exchange(x.reshape(pieces, -1, width), BOTH, groups), axis=0)

    def spread(x, pieces):
        return jnp.broadcast_to(x[None], (pieces,) + x.shape)

    in_plane, in_line = len(planes[0]), len(lines[0])
    mine = summed(keep, planes, in_plane)
    mine = summed(spread(mine, in_line), lines, in_line)
    return exchange(spread(mine, in_plane), BOTH, planes).reshape(count, width)


def shards(devices, n_dp, pair, upstream, residue_mask, w_in, w_gate, w_out, gains):
    _, rows, res, width = pair.shape
    hidden = w_out.shape[0]
    cells = rows * res
    n = devices // 2
    per = hidden // n
    same_core = [list(range(core, devices, 2)) for core in range(2)]
    pair2 = pair.reshape(cells, width)
    up2 = upstream.reshape(cells, width)
    tiles = n * 9 * per

    def wide(x):
        return exchange(x.reshape(n, 18 * per, 128), "dap", same_core).reshape(2 * tiles, 128)

    def narrow(x):
        return exchange(x.reshape(n, 9 * per, 128), "dap", same_core).reshape(tiles, 128)

    flat = (width, cells)
    product = 6 * width * hidden * cells

    send, zhat, zinv, val, sig = call(
        functools.partial(project_kernel, n, res),
        [((2 * tiles, 128), F32), (flat, F32), ((1, cells), F32), ((2 * hidden, cells), F32), ((2 * hidden, cells), F32)],
        [pltpu.VMEM((4 * hidden, 3 * width), BF16)],
    )(pair2, w_in, gains)
    got = wide(send)

    other = swap_cores(got.reshape(n * 9, 2, per, 128)[:, 1].reshape(tiles, 128), n)
    up2, _ = lax.optimization_barrier((up2, got))
    d_out, slope, grad = call(
        functools.partial(gate_kernel, res),
        [(flat, F32)] * 3,
        [pltpu.VMEM((2 * width, 2 * width), BF16), pltpu.VMEM((2 * hidden, 2 * width), BF16)],
        flops=2 * product,
        moved=4 * cells * width * 5,
    )(up2, zhat, w_gate, w_out, gains)
    other, d_out = lax.optimization_barrier((other, d_out))
    send, a_all, b_all, pm = call(
        functools.partial(triangle_kernel, n),
        [((tiles, 128), F32), ((per, res // 2, 256), F32), ((per * 512, 128), F32), ((512, 128), F32)],
        [pltpu.VMEM((8, 256), F32)],
    )(got, other, residue_mask)
    got = narrow(send)

    send, xhat = call(functools.partial(norm_back_kernel, n), [((tiles, 128), F32), (flat, F32)])(got, grad)
    got = narrow(send)

    keep, give = call(
        functools.partial(b_back_kernel, n, res),
        [((tiles, 128), F32)] * 2,
        [pltpu.VMEM((res // 2, 256), F32), pltpu.VMEM((512, 128), F32)],
    )(got, pm, a_all)
    give, got, xhat = lax.optimization_barrier((give, got, xhat))
    taken = swap_cores(give, n)
    (send,) = call(
        functools.partial(a_back_kernel, n, res),
        [((2 * tiles, 128), F32)],
        [pltpu.VMEM((res // 2, 256), F32)],
        flops=product,
        moved=4 * cells * width * 4,
    )(got, pm, b_all)
    dzn, mg, mo = call(
        output_kernel,
        [(flat, F32), ((width, width), F32), ((width, hidden), F32)],
        [pltpu.VMEM((2 * width, 2 * hidden), BF16), pltpu.VMEM((2 * width, 2 * width), BF16)],
        flops=4 * product,
        moved=4 * cells * width * 5,
    )(xhat, zhat, d_out, slope, w_gate, w_out, gains)
    taken, dzn, send = lax.optimization_barrier((taken, dzn, send))
    group = (n * 9, per, 128)
    (send,) = call(add_kernel, [((n * 9, 2 * per, 128), F32)])(
        send.reshape(n * 9, 2 * per, 128), keep.reshape(group), taken.reshape(group)
    )
    got = wide(send)

    half = (4 * hidden + 2 * width) // 2
    keep, give, d_hi, d_lo = call(
        functools.partial(weight_kernel, n),
        [((half, width), F32)] * 2 + [((4 * hidden, cells), BF16)] * 2,
        [pltpu.VMEM((4 * hidden, width), F32)],
    )(got, zhat, val, sig, mg, mo)
    taken = swap_cores(give, n)
    (d_pair,) = input_call(res, cells)(d_hi, d_lo, zhat, zinv, dzn, w_in, gains)
    taken, d_pair = lax.optimization_barrier((taken, d_pair))
    mine = reduce_all(keep + taken, n, n_dp)
    theirs = swap_cores(mine, n)

    d_w_in, d_w_gate, d_w_out, d_gains = call(
        finish_kernel,
        [(w_in.shape, F32), (w_gate.shape, F32), (w_out.shape, F32), (gains.shape, F32)],
        [pltpu.VMEM((2 * half, width), F32)],
    )(mine, theirs, w_in, w_gate, w_out, gains)
    return (d_pair.reshape(pair.shape), d_w_in, d_w_gate, d_w_out, d_gains)


def solution(mesh):
    cells = P("dp", "dap", None, None)
    in_specs = (cells, cells, P("dp", None), P(), P(), P(), P())
    out_specs = (cells, P(), P(), P(), P())
    body = functools.partial(shards, mesh.shape["dap"], mesh.shape["dp"])
    return jax.shard_map(body, mesh=mesh, in_specs=in_specs, out_specs=out_specs, check_vma=False)
```

```python
import functools

import jax
import jax.numpy as jnp
from jax import lax
from jax.experimental import pallas as pl
from jax.experimental.pallas import tpu as pltpu
from jax.sharding import PartitionSpec as P

F32 = jnp.float32
BF16 = jnp.bfloat16
LANES = 384
EPS = 1e-05


def parts(x):
    hi = x.astype(BF16)
    return hi, (x - hi.astype(F32)).astype(BF16)


def dot3(left, right, dims=((1,), (0,))):
    (ah, al), (bh, bl) = left, right

    def one(a, b):
        return lax.dot_general(a, b, (dims, ((), ())), preferred_element_type=F32)

    if dims == TN:
        return one(jnp.concatenate([ah, al], axis=0), jnp.concatenate([bh, bh], axis=0)) + one(ah, bl)
    both = one(jnp.concatenate([ah, al], axis=0), bh)
    m = ah.shape[0]
    return both[:m] + (both[m:] + one(ah, bl))


NT = ((1,), (1,))
TN = ((0,), (0,))


def stack_left(x):
    hi, lo = parts(x)
    return jnp.concatenate(
        [jnp.concatenate([hi, hi], axis=1), jnp.concatenate([lo, jnp.zeros_like(lo)], axis=1)], axis=0
    )


def stack_rows(x):
    return jnp.concatenate(parts(x), axis=0)


def dot_stacked(left, right):
    both = jnp.dot(left, right, preferred_element_type=F32)
    m = left.shape[0] // 2
    return both[:m] + both[m:]


def dot_cells(left, right):
    both = lax.dot_general(left, right, (NT, ((), ())), preferred_element_type=F32)
    m, n = left.shape[0] // 2, right.shape[0] // 2
    return both[:m, :n] + both[:m, n:] + both[m:, :n]


def column(row):
    n = row.shape[1]
    return jnp.broadcast_to(row, (n, n)).T[:, :1]


def hat(x):
    center = x - jnp.mean(x, axis=0, keepdims=True)
    inverse = lax.rsqrt(jnp.mean(center * center, axis=0, keepdims=True) + EPS)
    return center * inverse, inverse


def hat_back(g, xhat, inverse):
    first = jnp.mean(g, axis=0, keepdims=True)
    second = jnp.mean(g * xhat, axis=0, keepdims=True)
    return inverse * (g - first - xhat * second)


def call(body, outs, scratch=(), flops=0, moved=0):
    return pl.pallas_call(
        body,
        out_shape=[jax.ShapeDtypeStruct(s, d) for s, d in outs],
        scratch_shapes=list(scratch),
        compiler_params=pltpu.CompilerParams(vmem_limit_bytes=16 * 2**20),
        cost_estimate=pl.CostEstimate(flops=flops, bytes_accessed=moved, transcendentals=0),
    )


def cell_slices(c, res):
    base = c * 2 * res
    return (
        pl.ds(base, 128),
        pl.ds(base + 128, res - 128),
        pl.ds(base + res + 128, res - 128),
        pl.ds(base + res, 128),
    )


def load_cells(ref, c, res):
    return jnp.concatenate([ref[at, :] for at in cell_slices(c, res)], axis=0).T


def store_cells(ref, c, res, value):
    value = value.T
    start = 0
    for at in cell_slices(c, res):
        ref[at, :] = value[start : start + at.size, :]
        start += at.size


def tile_rows(n, kinds, tile, kind):
    return pl.ds(tile * kinds + kind, n, stride=9 * kinds)


def to_rows(tiles):
    return (tiles[0], tiles[1]), (tiles[2], pltpu.roll(tiles[1], 64, 1))


def to_tiles(even, odd):
    low = lax.broadcasted_iota(jnp.int32, even[1].shape, 1) < 64
    return even[0], jnp.where(low, even[1], pltpu.roll(odd[1], 64, 1)), odd[0]


def project_kernel(n, res, pair, w_in, send, zhat, zinv, val, sig, wt):
    hidden = w_in.shape[1] // 4
    per = hidden // n
    wh, wl = parts(w_in[...].T)
    wt[...] = jnp.concatenate([wh, wl, wh], axis=1)

    def step(c):
        at = pl.ds(c * LANES, LANES)
        z, inverse = hat(load_cells(pair, c, res))
        zhat[:, at] = z
        zinv[:, at] = inverse
        zh, zl = parts(z)
        zn = jnp.concatenate([zh, zh, zl], axis=0)
        for which in range(2):
            rows = pl.ds(2 * which * hidden, 2 * hidden)
            proj = jnp.dot(wt[rows, :], zn, preferred_element_type=F32)
            value, gate = proj[:hidden], jax.nn.sigmoid(proj[hidden:])
            val[pl.ds(which * hidden, hidden), at] = value
            sig[pl.ds(which * hidden, hidden), at] = gate
            both = value * gate
            for q in range(per):
                for t in range(3):
                    send[tile_rows(n, 2 * per, 3 * c + t, which * per + q), :] = both[
                        q * n : (q + 1) * n, t * 128 : (t + 1) * 128
                    ]

    for c in range(pair.shape[0] // LANES):
        step(c)


def make_masks(mask, line, swap):
    res = mask.shape[1]
    line[...] = jnp.zeros_like(line)
    line[0:1, pl.ds(0, res)] = mask[...].astype(F32)
    across = jnp.broadcast_to(line[0:1, :], (256, 256))
    both = across * across.T
    swap[0:256, :] = both[:, :128]
    swap[256:512, :] = both[:, 128:]


def read_masks(swap, n, res):
    rows = res // n
    return [[swap[pl.ds(256 * half + il, n, stride=rows), :] for half in range(2)] for il in range(rows)]


def core_of():
    return lax.rem(lax.axis_index("dap"), 2)


def by_core(mine, other):
    first = core_of() == 0
    return jnp.where(first, mine, other), jnp.where(first, other, mine)


def triangle_kernel(n, got, other, mask, send, a_out, b_out, swap, line):
    per = got.shape[0] // (2 * 9 * n)
    res = mask.shape[1]
    rows = res // (2 * n)
    make_masks(mask, line, swap)
    pm = read_masks(swap, n, res)
    for q in range(per):
        base = 512 * q
        for half in range(2):
            b_out[pl.ds(base + 256 * half + res, 256 - res), :] = jnp.zeros((256 - res, 128), F32)
        for p in range(rows // 2):
            two_a = to_rows([got[tile_rows(n, 2 * per, 3 * p + t, q), :] for t in range(3)])
            mine = [got[tile_rows(n, 2 * per, 3 * p + t, per + q), :] for t in range(3)]
            theirs = [other[tile_rows(n, per, 3 * p + t, q), :] for t in range(3)]
            tiles = [by_core(m, o) for m, o in zip(mine, theirs)]
            two_b = [to_rows([tile[core] for tile in tiles]) for core in range(2)]
            for side in range(2):
                il = 2 * p + side
                for half in range(2):
                    own = by_core(*[pm[core * rows + il][half] for core in range(2)])[0]
                    a_out[q, pl.ds(il * n, n), pl.ds(128 * half, 128)] = two_a[side][half] * own
                    for core in range(2):
                        row = core * rows + il
                        b_out[pl.ds(base + 256 * half + row, n, stride=2 * rows), :] = (
                            two_b[core][side][half] * pm[row][half]
                        )
        b_whole = jnp.concatenate([b_out[pl.ds(base, 256), :], b_out[pl.ds(base + 256, 256), :]], axis=1)
        x = dot3(parts(a_out[q]), parts(b_whole), NT)
        for p in range(rows // 2):
            even, odd = [
                [x[(2 * p + side) * n : (2 * p + side + 1) * n, 128 * half : 128 * half + 128] for half in range(2)]
                for side in range(2)
            ]
            for t, tile in enumerate(to_tiles(even, odd)):
                send[tile_rows(n, per, 3 * p + t, q), :] = tile


def gate_kernel(res, up, zhat, w_gate, w_out, gains, d_out, slope, grad, wgt, wo):
    gain0, gain1 = column(gains[0:1, :]), column(gains[1:2, :])
    wgt[...] = stack_left(w_gate[...].T)
    wo[...] = stack_left(w_out[...])

    def step(c):
        at = pl.ds(c * LANES, LANES)
        gate = jax.nn.sigmoid(dot_stacked(wgt[...], stack_rows(zhat[:, at] * gain0)))
        passed = load_cells(up, c, res) * gate
        d_out[:, at] = passed
        slope[:, at] = passed * (1.0 - gate)
        grad[:, at] = dot_stacked(wo[...], stack_rows(passed)) * gain1

    for c in range(up.shape[0] // LANES):
        step(c)


def norm_back_kernel(n, got, grad, send, xhat):
    per = got.shape[0] // (9 * n)

    def step(c):
        at = pl.ds(c * LANES, LANES)
        x = jnp.concatenate(
            [
                jnp.concatenate([got[tile_rows(n, per, 3 * c + t, q), :] for q in range(per)], axis=0)
                for t in range(3)
            ],
            axis=1,
        )
        normal, inverse = hat(x)
        xhat[:, at] = normal
        dx = hat_back(grad[:, at], normal, inverse)
        for q in range(per):
            for t in range(3):
                send[tile_rows(n, per, 3 * c + t, q), :] = dx[q * n : (q + 1) * n, t * 128 : (t + 1) * 128]

    for c in range(xhat.shape[1] // LANES):
        step(c)


def output_kernel(xhat, zhat, d_out, slope, w_gate, w_out, gains, dzn, mg, mo, wot, wg):
    gain1 = column(gains[1:2, :])
    wot[...] = stack_left(w_out[...].T)
    wg[...] = stack_left(w_gate[...])
    mg[...] = jnp.zeros_like(mg)
    mo[...] = jnp.zeros_like(mo)

    def step(c):
        at = pl.ds(c * LANES, LANES)
        normal = xhat[:, at]
        d_logit = stack_rows(slope[:, at] * dot_stacked(wot[...], stack_rows(normal * gain1)))
        mo[...] += dot_cells(stack_rows(d_out[:, at]), stack_rows(normal))
        mg[...] += dot_cells(d_logit, stack_rows(zhat[:, at]))
        dzn[:, at] = dot_stacked(wg[...], d_logit)

    for c in range(xhat.shape[1] // LANES):
        step(c)


def gather_dx(n, got, q, dx_all):
    per = got.shape[0] // (9 * n)
    for p in range(3):
        two = to_rows([got[tile_rows(n, per, 3 * p + t, q), :] for t in range(3)])
        for side in range(2):
            for half in range(2):
                dx_all[pl.ds((2 * p + side) * n, n), pl.ds(128 * half, 128)] = two[side][half]
    return parts(dx_all[...])


def b_back_kernel(n, res, got, swap, a_in, keep, give, dx_all, db_all):
    per = got.shape[0] // (9 * n)
    rows = res // (2 * n)
    pm = read_masks(swap, n, res)
    for q in range(per):
        db = dot3(gather_dx(n, got, q, dx_all), parts(a_in[q]), TN)
        db_all[0:256, :] = db[:, :128]
        db_all[256:512, :] = db[:, 128:]
        for p in range(rows // 2):
            tiles = []
            for core in range(2):
                two = []
                for row in (core * rows + 2 * p, core * rows + 2 * p + 1):
                    two.append(
                        [db_all[pl.ds(256 * half + row, n, stride=2 * rows), :] * pm[row][half] for half in range(2)]
                    )
                tiles.append(to_tiles(*two))
            for t in range(3):
                at = tile_rows(n, per, 3 * p + t, q)
                keep[at, :], give[at, :] = by_core(tiles[0][t], tiles[1][t])


def a_back_kernel(n, res, got, swap, b_in, send, dx_all):
    per = got.shape[0] // (9 * n)
    rows = res // (2 * n)
    pm = read_masks(swap, n, res)
    for q in range(per):
        base = 512 * q
        b_whole = jnp.concatenate([b_in[pl.ds(base, 256), :], b_in[pl.ds(base + 256, 256), :]], axis=1)
        da = dot3(gather_dx(n, got, q, dx_all), parts(b_whole))
        for p in range(rows // 2):
            two = []
            for il in (2 * p, 2 * p + 1):
                own = [by_core(pm[il][half], pm[rows + il][half])[0] for half in range(2)]
                two.append([da[il * n : (il + 1) * n, 128 * half : 128 * half + 128] * own[half] for half in range(2)])
            for t, tile in enumerate(to_tiles(*two)):
                send[tile_rows(n, 2 * per, 3 * p + t, q), :] = tile


def add_kernel(half_sent, keep, taken, send):
    per = keep.shape[1]
    send[:, :per, :] = half_sent[:, :per, :]
    send[:, per:, :] = keep[...] + taken[...]


def read_grads(n, got, val, sig, c, which):
    hidden = val.shape[0] // 2
    per = hidden // n
    at = pl.ds(c * LANES, LANES)
    d = jnp.concatenate(
        [
            jnp.concatenate([got[tile_rows(n, 2 * per, 3 * c + t, which * per + q), :] for q in range(per)], axis=0)
            for t in range(3)
        ],
        axis=1,
    )
    rows = pl.ds(which * hidden, hidden)
    gate = sig[rows, at]
    d_val = d * gate
    return d_val, d_val * val[rows, at] * (1.0 - gate)


def weight_kernel(n, got, zhat, val, sig, mg, mo, keep, give, d_hi, d_lo, mi):
    mi[...] = jnp.zeros_like(mi)

    def step(c):
        at = pl.ds(c * LANES, LANES)
        grads = [grad for which in range(2) for grad in read_grads(n, got, val, sig, c, which)]
        hi, lo = parts(jnp.concatenate(grads, axis=0))
        d_hi[:, at], d_lo[:, at] = hi, lo
        mi[...] += dot_cells(jnp.concatenate([hi, lo], axis=0), stack_rows(zhat[:, at]))

    for c in range(zhat.shape[1] // LANES):
        step(c)
    half = keep.shape[0]
    low = mi[pl.ds(0, half), :]
    high = jnp.concatenate([mi[pl.ds(half, mi.shape[0] - half), :], mg[...], mo[...]], axis=0)
    keep[...], give[...] = by_core(low, high)


def input_kernel(res, d_hi, d_lo, zhat, zinv, dzn, w_in, gains, d_pair, w_two, rows, sems):
    width = zhat.shape[0]
    w_two[...] = stack_rows(w_in[...])
    gain0 = column(gains[0:1, :])
    copies = []
    for c in range(rows.shape[0] // LANES):
        at = pl.ds(c * LANES, LANES)
        both = jnp.dot(w_two[...], d_hi[:, at], preferred_element_type=F32)
        total = both[:width] + both[width:] + jnp.dot(w_two[:width, :], d_lo[:, at], preferred_element_type=F32)
        store_cells(rows, c, res, hat_back((total + dzn[:, at]) * gain0, zhat[:, at], zinv[:, at]))
        copies.append(pltpu.make_async_copy(rows.at[at, :], d_pair.at[at, :], sems.at[c]))
        copies[-1].start()
    for copy in copies:
        copy.wait()


def finish_kernel(mine, theirs, w_in, w_gate, w_out, gains, d_w_in, d_w_gate, d_w_out, d_gains, m):
    width = w_out.shape[0]
    half = mine.shape[0]
    m[0:half, :], m[half:, :] = by_core(mine[...], theirs[...])
    gain0, gain1 = column(gains[0:1, :]), column(gains[1:2, :])
    fold = jnp.zeros((width, width), F32)
    for k in range(w_in.shape[1] // width):
        cols = pl.ds(k * width, width)
        part = m[cols, :].T
        d_w_in[:, cols] = part * gain0
        fold += part * w_in[:, cols]
    base = w_in.shape[1]
    part = m[pl.ds(base, width), :].T
    d_w_gate[...] = part * gain0
    fold += part * w_gate[...]
    d_gains[0:1, :] = jnp.sum(fold.T, axis=0, keepdims=True)
    part = m[pl.ds(base + width, width), :].T
    d_w_out[...] = part * gain1
    d_gains[1:2, :] = jnp.sum((part * w_out[...]).T, axis=0, keepdims=True)


def input_call(res, cells):
    def run(*operands):
        width = operands[2].shape[0]
        return pl.pallas_call(
            functools.partial(input_kernel, res),
            out_shape=[jax.ShapeDtypeStruct((cells, width), F32)],
            out_specs=[pl.BlockSpec(memory_space=pl.ANY)],
            scratch_shapes=[
                pltpu.VMEM((2 * width, operands[0].shape[0]), BF16),
                pltpu.VMEM((cells, width), F32),
                pltpu.SemaphoreType.DMA((cells // LANES,)),
            ],
            compiler_params=pltpu.CompilerParams(vmem_limit_bytes=16 * 2**20),
            cost_estimate=pl.CostEstimate(
                flops=24 * cells * width * width, bytes_accessed=28 * cells * width, transcendentals=0
            ),
        )(*operands)

    return run


def exchange(x, axis, groups):
    return lax.all_to_all(x, axis, 0, 0, tiled=True, axis_index_groups=groups)


def swap_cores(x, n):
    return lax.ppermute(x, "dap", [(i, i ^ 1) for i in range(2 * n)])


BOTH = ("dp", "dap")
NY = 4


def plane_and_line(n, n_dp):
    nx = max(1, n_dp // 2)
    nlo, nhi = n_dp // nx, n // NY

    def index(x, y, hi, lo, core):
        return (lo * nx + x) * 2 * n + (y * nhi + hi) * 2 + core

    planes = [
        [index(x, y, hi, lo, core) for x in range(nx) for y in range(NY)]
        for hi in range(nhi)
        for lo in range(nlo)
        for core in range(2)
    ]
    lines = [
        [index(x, y, hi, lo, core) for hi in range(nhi) for lo in range(nlo)]
        for x in range(nx)
        for y in range(NY)
        for core in range(2)
    ]
    return planes, lines


def reduce_all(keep, n, n_dp):
    planes, lines = plane_and_line(n, n_dp)
    count, width = keep.shape

    def summed(x, groups, pieces):
        return jnp.sum(exchange(x.reshape(pieces, -1, width), BOTH, groups), axis=0)

    def spread(x, pieces):
        return jnp.broadcast_to(x[None], (pieces,) + x.shape)

    in_plane, in_line = len(planes[0]), len(lines[0])
    mine = summed(keep, planes, in_plane)
    mine = summed(spread(mine, in_line), lines, in_line)
    return exchange(spread(mine, in_plane), BOTH, planes).reshape(count, width)


def shards(devices, n_dp, pair, upstream, residue_mask, w_in, w_gate, w_out, gains):
    _, rows, res, width = pair.shape
    hidden = w_out.shape[0]
    cells = rows * res
    n = devices // 2
    per = hidden // n
    same_core = [list(range(core, devices, 2)) for core in range(2)]
    pair2 = pair.reshape(cells, width)
    up2 = upstream.reshape(cells, width)
    tiles = n * 9 * per

    def wide(x):
        return exchange(x.reshape(n, 18 * per, 128), "dap", same_core).reshape(2 * tiles, 128)

    def narrow(x):
        return exchange(x.reshape(n, 9 * per, 128), "dap", same_core).reshape(tiles, 128)

    flat = (width, cells)
    product = 6 * width * hidden * cells

    send, zhat, zinv, val, sig = call(
        functools.partial(project_kernel, n, res),
        [((2 * tiles, 128), F32), (flat, F32), ((1, cells), F32), ((2 * hidden, cells), F32), ((2 * hidden, cells), F32)],
        [pltpu.VMEM((4 * hidden, 3 * width), BF16)],
    )(pair2, w_in * gains[0][:, None])
    got = wide(send)

    other = swap_cores(got.reshape(n * 9, 2, per, 128)[:, 1].reshape(tiles, 128), n)
    up2, _ = lax.optimization_barrier((up2, got))
    d_out, slope, grad = call(
        functools.partial(gate_kernel, res),
        [(flat, F32)] * 3,
        [pltpu.VMEM((2 * width, 2 * width), BF16), pltpu.VMEM((2 * hidden, 2 * width), BF16)],
        flops=2 * product,
        moved=4 * cells * width * 5,
    )(up2, zhat, w_gate, w_out, gains)
    other, d_out = lax.optimization_barrier((other, d_out))
    send, a_all, b_all, pm = call(
        functools.partial(triangle_kernel, n),
        [((tiles, 128), F32), ((per, res // 2, 256), F32), ((per * 512, 128), F32), ((512, 128), F32)],
        [pltpu.VMEM((8, 256), F32)],
    )(got, other, residue_mask)
    got = narrow(send)

    send, xhat = call(functools.partial(norm_back_kernel, n), [((tiles, 128), F32), (flat, F32)])(got, grad)
    got = narrow(send)

    keep, give = call(
        functools.partial(b_back_kernel, n, res),
        [((tiles, 128), F32)] * 2,
        [pltpu.VMEM((res // 2, 256), F32), pltpu.VMEM((512, 128), F32)],
    )(got, pm, a_all)
    give, got, xhat = lax.optimization_barrier((give, got, xhat))
    taken = swap_cores(give, n)
    (send,) = call(
        functools.partial(a_back_kernel, n, res),
        [((2 * tiles, 128), F32)],
        [pltpu.VMEM((res // 2, 256), F32)],
        flops=product,
        moved=4 * cells * width * 4,
    )(got, pm, b_all)
    dzn, mg, mo = call(
        output_kernel,
        [(flat, F32), ((width, width), F32), ((width, hidden), F32)],
        [pltpu.VMEM((2 * width, 2 * hidden), BF16), pltpu.VMEM((2 * width, 2 * width), BF16)],
        flops=4 * product,
        moved=4 * cells * width * 5,
    )(xhat, zhat, d_out, slope, w_gate, w_out, gains)
    taken, dzn, send = lax.optimization_barrier((taken, dzn, send))
    group = (n * 9, per, 128)
    (send,) = call(add_kernel, [((n * 9, 2 * per, 128), F32)])(
        send.reshape(n * 9, 2 * per, 128), keep.reshape(group), taken.reshape(group)
    )
    got = wide(send)

    half = (4 * hidden + 2 * width) // 2
    keep, give, d_hi, d_lo = call(
        functools.partial(weight_kernel, n),
        [((half, width), F32)] * 2 + [((4 * hidden, cells), BF16)] * 2,
        [pltpu.VMEM((4 * hidden, width), F32)],
    )(got, zhat, val, sig, mg, mo)
    taken = swap_cores(give, n)
    (d_pair,) = input_call(res, cells)(d_hi, d_lo, zhat, zinv, dzn, w_in, gains)
    taken, d_pair = lax.optimization_barrier((taken, d_pair))
    mine = reduce_all(keep + taken, n, n_dp)
    theirs = swap_cores(mine, n)

    d_w_in, d_w_gate, d_w_out, d_gains = call(
        finish_kernel,
        [(w_in.shape, F32), (w_gate.shape, F32), (w_out.shape, F32), (gains.shape, F32)],
        [pltpu.VMEM((2 * half, width), F32)],
    )(mine, theirs, w_in, w_gate, w_out, gains)
    return (d_pair.reshape(pair.shape), d_w_in, d_w_gate, d_w_out, d_gains)


def solution(mesh):
    cells = P("dp", "dap", None, None)
    in_specs = (cells, cells, P("dp", None), P(), P(), P(), P())
    out_specs = (cells, P(), P(), P(), P())
    body = functools.partial(shards, mesh.shape["dap"], mesh.shape["dp"])
    return jax.shard_map(body, mesh=mesh, in_specs=in_specs, out_specs=out_specs, check_vma=False)
```
